128 devices in a mesh: slab: 32 (over z, x, core), row: 4 (over y).
Axes of the slice: x: 4, y: 4, z: 4, core: 2. Of those that a mesh axis runs over, the one named last changes fastest.
Arguments:
- slot_brick: int32 [128, 128, 2], P(('slab', 'row')), may hold values from 0 to 255
- slot_count: int32 [128, 128, 2], P(('slab', 'row')), may hold values from 1 to 64, as said below
- point_cell: int32 [128, 128, 2, 64], P(('slab', 'row')), may hold values from 0 to 1023
- point_frac: float32 [128, 128, 2, 64], P(('slab', 'row')), may hold values from -0.5 to 0.5
- point_normal: float32 [128, 128, 2, 3, 64], P(('slab', 'row')), may hold values from -6 to 6
- point_weight: float32 [128, 128, 2, 64], P(('slab', 'row')), may hold values from 0.2 to 2
- guess: float32 [512, 64, 1024], P('slab', 'row'), may hold values from -4 to 4
Outputs:
- indicator: float32 [512, 64, 1024], P('slab', 'row')
The draws below stay inside these ranges and needn't reach their ends.
Inputs may be any that keep to these rules, and one draw needn't show every extreme that they name: `slot_count`: every source block has at least one slot with exactly 64 live points.
All inputs are finite; a program needn't handle non-finite values.
Results may differ from the reference program's by a relative error of at most 0.0003.
Values sent between devices are 32-bit elements; how exact they have to be, the bound alone decides.
A program may use at most 64 MiB of HBM per device.

```python
import math
import jax
import jax.numpy as jnp
from jax import lax

Z_DEV = 16
Y_DEV = 16
NX = 1024
CAP = 64
S_PEER = 2
SWEEPS = 3
NZ = 512
NY = 64
BRICKS_DEV = 256
N_ROW = 4
DEVICES = 128


def draw_slot_count(key, part):
    first, second = jax.random.split(jax.random.fold_in(key, 17))
    base = jax.random.randint(first, (DEVICES, DEVICES * S_PEER), 1, CAP + 1)
    chosen = jax.random.randint(second, (DEVICES,), 0, DEVICES * S_PEER)
    lanes = jnp.arange(DEVICES * S_PEER, dtype=jnp.int32)
    filled = jnp.where(lanes[None, :] == chosen[:, None], CAP, base)
    return filled.reshape(DEVICES, DEVICES, S_PEER).astype(jnp.int32)


def touch_ends(values, stream_key, low, top_value):
    spot = [jax.random.randint(jax.random.fold_in(stream_key, axis), (), 0, length) for axis, length in enumerate(values.shape)]
    main_axis = values.shape.index(max(values.shape))
    neighbour = spot[:main_axis] + [(spot[main_axis] + 1) % values.shape[main_axis]] + spot[main_axis + 1:]
    return values.at[tuple(spot)].set(low).at[tuple(neighbour)].set(top_value)


def steps_of(stream_key, dims, shards, least, top_value):
    def one(axis_at, blocks):
        steps = jax.random.uniform(jax.random.fold_in(jax.random.fold_in(stream_key, 6), axis_at), (blocks,), jnp.float32, least / len(shards), top_value / len(shards))
        return jnp.repeat(jnp.exp(steps), dims[axis_at] // blocks).reshape((-1,) + (1,) * (len(dims) - axis_at - 1))

    loudness = one(*shards[0])
    for cut in shards[1:]:
        loudness = loudness * one(*cut)
    return loudness


def bell_draw(rng, shape, width, bound, shards=(), kind=jnp.bfloat16):
    drawn = jax.random.normal(rng, shape, jnp.float32) * width
    if len(shards) > 0:
        drawn = steps_of(rng, shape, shards, -0.22, 0.18) * drawn
    return jnp.clip(drawn, min=-bound, max=bound).astype(kind)


def setup_inputs(seed: int = 0) -> dict:
    keys = jax.random.split(jax.random.key(seed), 8)
    slot_brick = touch_ends(jax.random.randint(keys[0], (DEVICES, DEVICES, S_PEER), 0, BRICKS_DEV), jax.random.fold_in(keys[0], 1), 0, BRICKS_DEV - 1).astype(jnp.int32)
    slot_count = draw_slot_count(jax.random.fold_in(keys[7], 71), 0)
    point_cell = touch_ends(jax.random.randint(keys[2], (DEVICES, DEVICES, S_PEER, CAP), 0, NX), jax.random.fold_in(keys[2], 1), 0, NX - 1).astype(jnp.int32)
    point_frac = jnp.clip(jax.random.uniform(keys[3], (DEVICES, DEVICES, S_PEER, CAP), jnp.float32, -0.5, 0.5) * steps_of(keys[3], (DEVICES, DEVICES, S_PEER, CAP), ((0, 128),), -0.4, 0.0), -0.5, 0.5)
    point_normal = bell_draw(keys[4], (DEVICES, DEVICES, S_PEER, 3, CAP), 1.0, 6.0, ((0, 128),), jnp.float32)
    point_weight = jnp.clip(jnp.exp(math.log(2.0) - 2.3025851 * jax.random.uniform(keys[5], (DEVICES, DEVICES, S_PEER, CAP), jnp.float32) ** steps_of(keys[5], (DEVICES, DEVICES, S_PEER, CAP), ((0, 128),), -0.2, 0.2)), 0.2, 2.0)
    guess = bell_draw(keys[6], (NZ, NY, NX), 0.5, 4.0, ((0, 32), (1, 4)), jnp.float32)
    return dict(slot_brick=slot_brick, slot_count=slot_count, point_cell=point_cell, point_frac=point_frac, point_normal=point_normal, point_weight=point_weight, guess=guess)


HIGH = lax.Precision.HIGHEST
ALPHA = 4.0


def splat_block(cell, frac, count, values):
    lanes = jnp.arange(cell.shape[1], dtype=jnp.int32)
    live = (lanes[None, :] < count[:, None]).astype(jnp.float32)
    low = 0.5 * (0.5 - frac) ** 2 * live
    middle = (0.75 - frac * frac) * live
    high = 0.5 * (0.5 + frac) ** 2 * live
    cells = jnp.arange(NX, dtype=jnp.int32)
    delta = cells[None, None, :] - cell[:, :, None]
    table = jnp.where(delta == -1, low[..., None], jnp.where(delta == 0, middle[..., None], jnp.where(delta == 1, high[..., None], jnp.float32(0.0))))
    return jnp.einsum("nkp,npx->nkx", values, table, precision=HIGH)


def along(array, axis, kind):
    size = array.shape[axis] - 2
    lower = lax.slice_in_dim(array, 0, size, axis=axis)
    centre = lax.slice_in_dim(array, 1, size + 1, axis=axis)
    upper = lax.slice_in_dim(array, 2, size + 2, axis=axis)
    if kind == "mass":
        return (lower + 4.0 * centre + upper) / 6.0
    return 2.0 * centre - lower - upper


def stiffness(padded):
    mass_x = along(padded, 2, "mass")
    stiff_x = along(padded, 2, "stiff")
    return (along(along(mass_x, 1, "mass"), 0, "stiff") + along(along(mass_x, 1, "stiff"), 0, "mass")
            + along(along(stiff_x, 1, "mass"), 0, "mass"))


def reference(slot_brick, slot_count, point_cell, point_frac, point_normal, point_weight, guess):
    total = DEVICES * DEVICES * S_PEER
    block = 64
    dest = jnp.broadcast_to(jnp.arange(DEVICES, dtype=jnp.int32)[None, :, None], slot_brick.shape)
    global_z = (dest // N_ROW) * Z_DEV + slot_brick // Y_DEV
    global_y = (dest % N_ROW) * Y_DEV + slot_brick % Y_DEV
    target = (global_z * NY + global_y).reshape(total // block, block)
    cells = point_cell.reshape(total // block, block, CAP)
    fracs = point_frac.reshape(total // block, block, CAP)
    counts = slot_count.reshape(total // block, block)
    values = jnp.concatenate([point_normal, point_weight[:, :, :, None, :]], axis=3).reshape(total // block, block, 4, CAP)

    def step(field, item):
        where, cell, frac, count, value = item
        return field.at[where].add(splat_block(cell, frac, count, value)), None

    start = jnp.zeros((NZ * NY, 4, NX), jnp.float32)
    field, _ = lax.scan(step, start, (target, cells, fracs, counts, values))
    field = jnp.transpose(field.reshape(NZ, NY, 4, NX), (2, 0, 1, 3))
    padded = jnp.pad(field[0:3], ((0, 0), (1, 1), (1, 1), (1, 1)))
    spread = (padded[0, 1:-1, 1:-1, 2:] - padded[0, 1:-1, 1:-1, :-2]
              + padded[1, 1:-1, 2:, 1:-1] - padded[1, 1:-1, :-2, 1:-1]
              + padded[2, 2:, 1:-1, 1:-1] - padded[2, :-2, 1:-1, 1:-1])
    rhs = -0.5 * spread
    density = field[3]
    inverse = 1.0 / (8.0 / 3.0 + ALPHA * density)
    parity = (jnp.arange(NZ, dtype=jnp.int32)[:, None, None] + jnp.arange(NY, dtype=jnp.int32)[None, :, None]
              + jnp.arange(NX, dtype=jnp.int32)[None, None, :]) % 2
    indicator = guess
    for sweep in range(SWEEPS):
        for colour in (0, 1):
            mask = (parity == colour).astype(jnp.float32)
            residue = rhs - stiffness(jnp.pad(indicator, 1)) - ALPHA * density * indicator
            indicator = indicator + mask * residue * inverse
    return indicator
```

```python
import functools

import jax
import jax.numpy as jnp
from jax import lax
from jax.experimental import pallas as pl
from jax.experimental.pallas import tpu as pltpu
from jax.sharding import PartitionSpec as P

Z_DEV = 16
Y_DEV = 16
NX = 1024
CAP = 64
S_PEER = 2
SWEEPS = 3
HALF = Z_DEV // 2
TILE = (8, 128)
MESH = pl.DeviceIdType.MESH
F32 = jnp.float32
BF16 = jnp.bfloat16
I32 = jnp.int32


def iota(shape, dim):
    return lax.broadcasted_iota(I32, shape, dim)


def swap_halves(tiles):
    return pltpu.roll(tiles, 4, tiles.ndim - 2)


def low_half(shape):
    return iota(shape, len(shape) - 2) < 4


def neighbour(tiles, parity):
    shape = tiles.shape
    lane, sub = iota(shape, len(shape) - 1), iota(shape, len(shape) - 2) % 4
    if parity == 0:
        near = pltpu.roll(tiles, 1, len(shape) - 1)
        far = pltpu.roll(near, 1, len(shape) - 2)
        edge, end = lane == 0, sub == 0
    else:
        near = pltpu.roll(tiles, 127, len(shape) - 1)
        far = pltpu.roll(near, 7, len(shape) - 2)
        edge, end = lane == 127, sub == 3
    return jnp.where(edge, jnp.where(end, 0.0, far), near)


def by_rows(tiles, parity, function):
    pairs = tiles.reshape(tiles.shape[0] // 2, 2, *TILE)
    done = [function(pairs[:, q], (parity + q) % 2) for q in range(2)]
    return jnp.stack(done, axis=1).reshape(tiles.shape)


def parts(x):
    high = x.astype(BF16)
    return high, (x - high.astype(F32)).astype(BF16)


def pack_kernel(brick_ref, count_ref, cell_ref, frac_ref, normal_ref, weight_ref, out_ref):
    lane = iota((cell_ref.shape[0], CAP), 1)

    def rows(first, second):
        return jnp.concatenate([first, second], axis=1)

    live = rows(*[(lane < count_ref[:, s : s + 1]).astype(F32) for s in range(S_PEER)])
    out_ref[:, 0, :] = rows(cell_ref[:, 0, :], cell_ref[:, 1, :]).astype(F32)
    out_ref[:, 1, :] = rows(frac_ref[:, 0, :], frac_ref[:, 1, :])
    for ch in range(3):
        out_ref[:, 2 + ch, :] = rows(normal_ref[:, 0, ch, :], normal_ref[:, 1, ch, :]) * live
    out_ref[:, 5, :] = rows(weight_ref[:, 0, :], weight_ref[:, 1, :]) * live
    bricks = rows(*[jnp.broadcast_to(brick_ref[:, s : s + 1], lane.shape) for s in range(S_PEER)]).astype(F32)
    out_ref[:, 6, :] = bricks
    out_ref[:, 7, :] = bricks


def deinterleave(guess_ref, start_ref):
    col, row = iota((256, 256), 1), iota((256, 256), 0)
    place = (row == jnp.where(col < 128, 2 * col, 2 * col - 255)).astype(BF16)
    rows = Z_DEV * Y_DEV
    cells = iota((rows, 128), 0)
    even = (cells + cells // Y_DEV) % 2 == 0
    for i in range(4):
        chunk = guess_ref[:, :, 256 * i : 256 * (i + 1)].reshape(rows, 256)
        high, low = parts(chunk)
        split = jnp.dot(high, place, preferred_element_type=F32) + jnp.dot(low, place, preferred_element_type=F32)
        first, second = split[:, :128], split[:, 128:]
        colours = (jnp.where(even, first, second), jnp.where(even, second, first))
        for colour in range(2):
            for z in range(Z_DEV):
                base = ((colour * HALF + z % HALF) * Y_DEV) * 8 + (z // HALF) * 4 + i
                start_ref[pl.ds(base, Y_DEV, stride=8), :] = colours[colour][z * Y_DEV : (z + 1) * Y_DEV]


def splat_kernel(points_ref, guess_ref, rhs_ref, inv_ref, yface_ref, zface_ref, start_ref, acc, brick_v, brick_s, f1, f2, sem):
    sources = points_ref.shape[0] // 8
    brick_v[...] = points_ref[pl.ds(6, sources, stride=8), :].astype(I32)
    copy = pltpu.make_async_copy(brick_v, brick_s, sem)
    copy.start()

    def clear(b, _):
        acc[pl.ds(b * 8, 8)] = jnp.zeros((8, 32, 128), F32)
        return 0

    lax.fori_loop(0, Z_DEV * Y_DEV // 8, clear, 0)
    deinterleave(guess_ref, start_ref)
    copy.wait()

    lane = iota(TILE, 1)
    left = lane < CAP
    rank = iota(TILE, 0)
    wide_rank = iota((128, 128), 0)

    def group(g, _):
        cell, frac, n0, n1, n2, w, brick = [points_ref[pl.ds(g * 64 + r, 8, stride=8), :] for r in range(7)]
        cell, brick = cell.astype(I32), brick.astype(I32)
        parity, k = cell & 1, cell >> 1
        even = parity == 0
        wl = 0.5 * (0.5 - frac) * (0.5 - frac)
        wm = 0.75 - frac * frac
        wh = 0.5 * (0.5 + frac) * (0.5 + frac)
        beside = jnp.where(even, wh, wl)
        beyond = jnp.where(even, wl, wh)
        k2 = jnp.where(even, k - 1, k + 1)
        zl, yl = brick >> 4, brick & 15
        side = (parity + zl + yl + (zl >> 3)) & 1
        h1 = side * 4 + (k >> 7)
        h2 = (1 - side) * 4 + (k >> 7)
        inside = (k2 >= 0) & (k2 < NX // 2)
        h3 = jnp.where(inside, (1 - side) * 4 + (k2 >> 7), -1)
        none = jnp.full(TILE, -1, I32)
        zero = jnp.zeros(TILE, F32)

        def swap(x):
            return pltpu.roll(x, 64, 1)

        def both(x, y):
            return (jnp.where(left, x, swap(y)), jnp.where(left, swap(x), y))

        lanes_ = both(k & 127, k2 & 127)
        ha, hb = both(h1, h3), both(h2, none)
        wa, wb = both(wm, beyond), both(beside, zero)
        vals = [both(v, v) for v in (n0, n1, n2, w)]
        for r in range(8):
            for s in range(S_PEER):
                def row(x):
                    return x[s][r : r + 1, :]

                unit = jnp.where(rank == row(ha), row(wa), jnp.where(rank == row(hb), row(wb), 0.0))
                a = jnp.concatenate([unit * row(v) for v in vals], axis=0)
                onehot = (wide_rank == row(lanes_)).astype(F32).astype(BF16)
                out = lax.dot_general(
                    jnp.concatenate(parts(a), axis=0), onehot, (((1,), (1,)), ((), ())), preferred_element_type=F32
                )
                b = brick_s[g * 8 + r, s * CAP]
                acc[b] = acc[b] + (out[:32] + out[32:])
        return 0

    lax.fori_loop(0, sources // 8, group, 0)

    low = low_half((Y_DEV, *TILE))

    def fields(zp, ch):
        one = acc[pl.ds(zp * Y_DEV, Y_DEV), ch * 8 : ch * 8 + 8, :]
        two = acc[pl.ds((zp + HALF) * Y_DEV, Y_DEV), ch * 8 : ch * 8 + 8, :]
        return jnp.where(low, one, two), swap_halves(jnp.where(low, two, one))

    nil = jnp.zeros((1, *TILE), F32)
    for colour in range(2):
        for zp in range(HALF):
            f1[colour, zp, 0:1] = nil
            f1[colour, zp, Y_DEV + 1 : Y_DEV + 2] = nil

    def planes(pair, _):
        for odd in range(2):
            zp = pair * 2 + odd
            x = fields(zp, 0)
            y = fields(zp, 1)
            z = fields(zp, 2)
            d = fields(zp, 3)
            for colour in range(2):
                def slope(tiles, parity):
                    other = neighbour(tiles, parity)
                    return tiles - other if parity == 0 else other - tiles

                rhs_ref[colour, zp] = by_rows(x[1 - colour], (odd + colour) % 2, slope)
                f1[colour, zp, 1 : Y_DEV + 1] = y[colour]
                f2[colour, zp + 1] = z[colour]
                inv_ref[colour, zp] = 1.0 / (32.0 + 48.0 * d[colour])
                yface_ref[0, colour, zp] = y[colour][0]
                yface_ref[1, colour, zp] = y[colour][Y_DEV - 1]
        return 0

    lax.fori_loop(0, HALF // 2, planes, 0)
    zface_ref[0] = acc[0:Y_DEV, 16:24, :]
    zface_ref[1] = acc[(Z_DEV - 1) * Y_DEV :, 16:24, :]
    for colour in range(2):
        f2[colour, 0] = swap_halves(jnp.where(low, f2[colour, HALF], 0.0))
        f2[colour, HALF + 1] = swap_halves(jnp.where(low, 0.0, f2[colour, 1]))

    def finish(zp, _):
        for colour in range(2):
            o = 1 - colour
            spread = rhs_ref[colour, zp] + f1[o, zp, 2:] - f1[o, zp, :-2] + f2[o, zp + 2] - f2[o, zp]
            rhs_ref[colour, zp] = -6.0 * spread
        return 0

    lax.fori_loop(0, HALF, finish, 0)


def relax_kernel(rhs_in, inv_ref, start_ref, yface_ref, zface_ref, out_ref, v, zin, rhs, yin, zfin, send, recv, fsend, frecv):
    ns, nr = lax.axis_size("slab"), lax.axis_size("row")
    slab, line = lax.axis_index("slab"), lax.axis_index("row")
    last = Y_DEV + 1
    sides = [(1, 0), (-1, 0), (0, 1), (0, -1), (1, 1), (1, -1), (-1, 1), (-1, -1)]

    def exists(d):
        ok = True
        for step, at, size in ((d[0], slab, ns), (d[1], line, nr)):
            if step == 1:
                ok = (at < size - 1) if ok is True else ok & (at < size - 1)
            if step == -1:
                ok = (at > 0) if ok is True else ok & (at > 0)
        return ok

    def device(d):
        return (slab + d[0], line + d[1])

    nil = jnp.zeros((1, *TILE), F32)
    for n in range(7):
        for s in range(2):
            zin[n, s] = jnp.zeros((Y_DEV + 2, *TILE), F32)
        for zp in range(HALF):
            v[n, zp + 1, 0:1] = nil
            v[n, zp + 1, last:] = nil
    yin[...] = jnp.zeros(yin.shape, F32)
    zfin[...] = jnp.zeros(zfin.shape, F32)

    barrier = pltpu.get_barrier_semaphore()
    for d in sides:
        @pl.when(exists(d))
        def _():
            pl.semaphore_signal(barrier, inc=1, device_id=device(d), device_id_type=MESH)
    for colour in range(2):
        for zp in range(HALF):
            v[colour, zp + 1, 1:last] = start_ref[colour, zp]
    counts = [1 + (at > 0).astype(I32) + (at < size - 1).astype(I32) for at, size in ((slab, ns), (line, nr))]
    pl.semaphore_wait(barrier, counts[0] * counts[1] - 1)

    def copies(n):
        spans = {0: (pl.ds(1, Y_DEV), pl.ds(1, Y_DEV)), 1: (pl.ds(Y_DEV, 1), pl.ds(0, 1)), -1: (pl.ds(1, 1), pl.ds(last, 1))}
        for q, d in enumerate(sides):
            src_y, dst_y = spans[d[1]]
            if d[0] == 0:
                src, dst = v.at[n, pl.ds(1, HALF), src_y], v.at[n, pl.ds(1, HALF), dst_y]
            else:
                src, dst = v.at[n, HALF if d[0] == 1 else 1, src_y], zin.at[n, 0 if d[0] == 1 else 1, dst_y]
            yield d, pltpu.make_async_remote_copy(src, dst, send.at[n, q], recv.at[n, q], device(d), MESH)

    def face_copies():
        for q, d in enumerate(sides[:4]):
            s = 0 if d[q // 2] == 1 else 1
            if d[0] == 0:
                src, dst = yface_ref.at[1 - s], yin.at[s]
            else:
                src, dst = zface_ref.at[1 - s], zfin.at[s]
            yield d, pltpu.make_async_remote_copy(src, dst, fsend.at[q], frecv.at[q], device(d), MESH)

    def start_all(pairs):
        for d, copy in pairs:
            @pl.when(exists(d))
            def _():
                copy.start()

    def take_all(pairs):
        for d, copy in pairs:
            @pl.when(exists((-d[0], -d[1])))
            def _():
                copy.wait_recv()

    def sent_all(pairs):
        for d, copy in pairs:
            @pl.when(exists(d))
            def _():
                copy.wait_send()

    def rims(n):
        low = low_half((Y_DEV + 2, *TILE))
        v[n, 0] = swap_halves(jnp.where(low, v[n, HALF], zin[n, 0]))
        v[n, HALF + 1] = swap_halves(jnp.where(low, zin[n, 1], v[n, 1]))

    start_all(face_copies())
    start_all(copies(0))
    start_all(copies(1))
    take_all(face_copies())
    low = low_half((Y_DEV, *TILE))
    for colour in range(2):
        for zp in range(HALF):
            rhs[colour, zp] = rhs_in[colour, zp]
        for zp in range(HALF):
            rhs[colour, zp, 0] += 6.0 * yin[0, 1 - colour, zp]
            rhs[colour, zp, Y_DEV - 1] -= 6.0 * yin[1, 1 - colour, zp]
        below, above = zfin[0], zfin[1]
        if colour == 1:
            below, above = swap_halves(below), swap_halves(above)
        rhs[colour, 0] += jnp.where(low, 6.0 * below, 0.0)
        rhs[colour, HALF - 1] -= jnp.where(low, 0.0, 6.0 * above)
    for n in range(2):
        take_all(copies(n))
        rims(n)

    for step in range(2 * SWEEPS):
        same, opp, new, colour = step, step + 1, step + 2, step % 2

        def planes(pair, _):
            for odd in range(2):
                zp = pair * 2 + odd
                s1 = v[same, zp] + v[same, zp + 2]
                o1 = v[opp, zp] + v[opp, zp + 2]
                s0 = v[same, zp + 1]
                faces = s1[1:last] + s0[:-2] + s0[2:]
                diagonal = s1[:-2] + s1[2:]
                across = 2.0 * faces + (o1[:-2] + o1[2:])
                total = rhs[colour, zp] + 2.0 * diagonal + across
                value = (total + by_rows(across, (odd + colour) % 2, neighbour)) * inv_ref[colour, zp]
                if step < 2 * SWEEPS - 1:
                    v[new, zp + 1, 1:last] = value
                if step == 2 * SWEEPS - 2:
                    out_ref[0, zp] = value
                if step == 2 * SWEEPS - 1:
                    out_ref[1, zp] = value
            return 0

        lax.fori_loop(0, HALF // 2, planes, 0)
        if step < 2 * SWEEPS - 1:
            start_all(copies(new))
            take_all(copies(new))
            rims(new)

    sent_all(face_copies())
    for n in range(2 * SWEEPS + 1):
        sent_all(copies(n))


def interleave_kernel(in_ref, out_ref):
    col, row = iota((256, 256), 1), iota((256, 256), 0)
    place = (col == jnp.where(row < 128, 2 * row, 2 * row - 255)).astype(BF16)
    rows = Z_DEV * Y_DEV
    cells = iota((rows, 128), 0)
    even = (cells + cells // Y_DEV) % 2 == 0
    for i in range(4):
        colours = []
        for colour in range(2):
            base = [((colour * HALF + z % HALF) * Y_DEV) * 8 + (z // HALF) * 4 + i for z in range(Z_DEV)]
            colours.append(jnp.concatenate([in_ref[pl.ds(b, Y_DEV, stride=8), :] for b in base], axis=0))
        red, black = colours
        both = jnp.concatenate([jnp.where(even, red, black), jnp.where(even, black, red)], axis=1)
        high, low = parts(both)
        merged = jnp.dot(high, place, preferred_element_type=F32) + jnp.dot(low, place, preferred_element_type=F32)
        out_ref[:, :, 256 * i : 256 * (i + 1)] = merged.reshape(Z_DEV, Y_DEV, 256)


VM = pl.BlockSpec(memory_space=pltpu.VMEM)


def call(kernel, outs, scratch, count, limit, **params):
    return pl.pallas_call(
        kernel,
        out_shape=outs,
        in_specs=[VM] * count,
        out_specs=jax.tree.map(lambda _: VM, outs),
        scratch_shapes=scratch,
        compiler_params=pltpu.CompilerParams(vmem_limit_bytes=limit << 20, **params),
    )


def shards(slot_brick, slot_count, point_cell, point_frac, point_normal, point_weight, guess):
    peers = point_cell.shape[1]
    full = jax.ShapeDtypeStruct((2, HALF, Y_DEV, *TILE), F32)
    sent = call(pack_kernel, jax.ShapeDtypeStruct((peers, 8, 128), F32), [], 6, 16)(
        slot_brick[0], slot_count[0], point_cell[0], point_frac[0], point_normal[0], point_weight[0]
    )
    points = lax.all_to_all(sent, ("slab", "row"), split_axis=0, concat_axis=0, tiled=True)
    outs = (
        full,
        full,
        jax.ShapeDtypeStruct((2, 2, HALF, *TILE), F32),
        jax.ShapeDtypeStruct((2, Y_DEV, *TILE), F32),
        jax.ShapeDtypeStruct((2 * HALF * Y_DEV * 8, 128), F32),
    )
    rhs, inv, yface, zface, start = call(
        splat_kernel,
        outs,
        [
            pltpu.VMEM((Z_DEV * Y_DEV, 32, 128), F32),
            pltpu.VMEM((peers, 128), I32),
            pltpu.SMEM((peers, 128), I32),
            pltpu.VMEM((2, HALF, Y_DEV + 2, *TILE), F32),
            pltpu.VMEM((2, HALF + 2, Y_DEV, *TILE), F32),
            pltpu.SemaphoreType.DMA,
        ],
        2,
        32,
    )(points.reshape(peers * 8, 128), guess)
    relaxed = call(
        relax_kernel,
        full,
        [
            pltpu.VMEM((7, HALF + 2, Y_DEV + 2, *TILE), F32),
            pltpu.VMEM((7, 2, Y_DEV + 2, *TILE), F32),
            pltpu.VMEM((2, HALF, Y_DEV, *TILE), F32),
            pltpu.VMEM((2, 2, HALF, *TILE), F32),
            pltpu.VMEM((2, Y_DEV, *TILE), F32),
            pltpu.SemaphoreType.DMA((7, 8)),
            pltpu.SemaphoreType.DMA((7, 8)),
            pltpu.SemaphoreType.DMA((4,)),
            pltpu.SemaphoreType.DMA((4,)),
        ],
        5,
        32,
        collective_id=0,
        has_side_effects=True,
    )(rhs, inv, start.reshape(full.shape), yface, zface)
    return call(interleave_kernel, jax.ShapeDtypeStruct((Z_DEV, Y_DEV, NX), F32), [], 1, 16)(relaxed.reshape(-1, 128))


def solution(mesh):
    placed = (
        P(("slab", "row"), None, None),
        P(("slab", "row"), None, None),
        P(("slab", "row"), None, None, None),
        P(("slab", "row"), None, None, None),
        P(("slab", "row"), None, None, None, None),
        P(("slab", "row"), None, None, None),
        P("slab", "row", None),
    )
    return jax.shard_map(
        shards, mesh=mesh, in_specs=placed, out_specs=P("slab", "row", None), check_vma=False
    )
```

```python
import functools

import jax
import jax.numpy as jnp
from jax import lax
from jax.experimental import pallas as pl
from jax.experimental.pallas import tpu as pltpu
from jax.sharding import PartitionSpec as P

Z_DEV = 16
Y_DEV = 16
NX = 1024
CAP = 64
S_PEER = 2
SWEEPS = 3
HALF = Z_DEV // 2
TILE = (8, 128)
MESH = pl.DeviceIdType.MESH
F32 = jnp.float32
BF16 = jnp.bfloat16
I32 = jnp.int32


def iota(shape, dim):
    return lax.broadcasted_iota(I32, shape, dim)


def swap_halves(tiles):
    return pltpu.roll(tiles, 4, tiles.ndim - 2)


def low_half(shape):
    return iota(shape, len(shape) - 2) < 4


def neighbour(tiles, parity):
    shape = tiles.shape
    lane, sub = iota(shape, len(shape) - 1), iota(shape, len(shape) - 2) % 4
    if parity == 0:
        near = pltpu.roll(tiles, 1, len(shape) - 1)
        far = pltpu.roll(near, 1, len(shape) - 2)
        edge, end = lane == 0, sub == 0
    else:
        near = pltpu.roll(tiles, 127, len(shape) - 1)
        far = pltpu.roll(near, 7, len(shape) - 2)
        edge, end = lane == 127, sub == 3
    return jnp.where(edge, jnp.where(end, 0.0, far), near)


def by_rows(tiles, parity, function):
    pairs = tiles.reshape(tiles.shape[0] // 2, 2, *TILE)
    done = [function(pairs[:, q], (parity + q) % 2) for q in range(2)]
    return jnp.stack(done, axis=1).reshape(tiles.shape)


def parts(x):
    high = x.astype(BF16)
    return high, (x - high.astype(F32)).astype(BF16)


def deinterleave(guess_ref, start_ref):
    col, row = iota((256, 256), 1), iota((256, 256), 0)
    place = (row == jnp.where(col < 128, 2 * col, 2 * col - 255)).astype(BF16)
    rows = Z_DEV * Y_DEV
    cells = iota((rows, 128), 0)
    even = (cells + cells // Y_DEV) % 2 == 0
    for i in range(4):
        chunk = guess_ref[:, :, 256 * i : 256 * (i + 1)].reshape(rows, 256)
        high, low = parts(chunk)
        split = jnp.dot(high, place, preferred_element_type=F32) + jnp.dot(low, place, preferred_element_type=F32)
        first, second = split[:, :128], split[:, 128:]
        colours = (jnp.where(even, first, second), jnp.where(even, second, first))
        for colour in range(2):
            for z in range(Z_DEV):
                base = ((colour * HALF + z % HALF) * Y_DEV) * 8 + (z // HALF) * 4 + i
                start_ref[pl.ds(base, Y_DEV, stride=8), :] = colours[colour][z * Y_DEV : (z + 1) * Y_DEV]


SIDES = [(0, 1), (0, -1), (1, 0), (-1, 0), (1, 1), (1, -1), (-1, 1), (-1, -1)]
LAST = Y_DEV + 1
RIM = (HALF + 2, Y_DEV + 2, *TILE)


class Grid:
    def __init__(self):
        self.ns, self.nr = lax.axis_size("slab"), lax.axis_size("row")
        self.slab, self.line = lax.axis_index("slab"), lax.axis_index("row")

    def exists(self, d):
        tests = []
        for step, at, size in ((d[0], self.slab, self.ns), (d[1], self.line, self.nr)):
            if step == 1:
                tests.append(at < size - 1)
            if step == -1:
                tests.append(at > 0)
        return tests[0] if len(tests) == 1 else tests[0] & tests[1]

    def device(self, d):
        return (self.slab + d[0], self.line + d[1])

    def greet_neighbours(self):
        barrier = pltpu.get_barrier_semaphore()
        for d in SIDES:
            @pl.when(self.exists(d))
            def _():
                pl.semaphore_signal(barrier, inc=1, device_id=self.device(d), device_id_type=MESH)

    def await_neighbours(self):
        counts = [
            1 + (at > 0).astype(I32) + (at < size - 1).astype(I32)
            for at, size in ((self.slab, self.ns), (self.line, self.nr))
        ]
        pl.semaphore_wait(pltpu.get_barrier_semaphore(), counts[0] * counts[1] - 1)

    def start(self, pairs):
        for d, copy in pairs:
            @pl.when(self.exists(d))
            def _():
                copy.start()

    def take(self, pairs):
        for d, copy in pairs:
            @pl.when(self.exists((-d[0], -d[1])))
            def _():
                copy.wait_recv()

    def sent(self, pairs):
        for d, copy in pairs:
            @pl.when(self.exists(d))
            def _():
                copy.wait_send()

    def clear_outside(self, tiles, edge):
        for d in SIDES:
            @pl.when(jnp.logical_not(self.exists((-d[0], -d[1]))))
            def _():
                if d[0] == 0:
                    y = 0 if d[1] == 1 else LAST
                    tiles[1 : HALF + 1, y : y + 1] = jnp.zeros((HALF, 1, *TILE), F32)
                else:
                    at, size = {0: (1, Y_DEV), 1: (0, 1), -1: (LAST, 1)}[d[1]]
                    edge[0 if d[0] == 1 else 1, at : at + size] = jnp.zeros((size, *TILE), F32)

    def halo(self, tiles, edge, send, recv):
        spans = {0: (pl.ds(1, Y_DEV), pl.ds(1, Y_DEV)), 1: (pl.ds(Y_DEV, 1), pl.ds(0, 1)), -1: (pl.ds(1, 1), pl.ds(LAST, 1))}
        pairs = []
        for q, d in enumerate(SIDES):
            src_y, dst_y = spans[d[1]]
            if d[0] == 0:
                src, dst = tiles.at[pl.ds(1, HALF), src_y], tiles.at[pl.ds(1, HALF), dst_y]
            else:
                src, dst = tiles.at[HALF if d[0] == 1 else 1, src_y], edge.at[0 if d[0] == 1 else 1, dst_y]
            pairs.append((d, pltpu.make_async_remote_copy(src, dst, send.at[q], recv.at[q], self.device(d), MESH)))
        return pairs


def rims(tiles, edge):
    low = low_half((Y_DEV + 2, *TILE))
    tiles[0] = swap_halves(jnp.where(low, tiles[HALF], edge[0]))
    tiles[HALF + 1] = swap_halves(jnp.where(low, edge[1], tiles[1]))


def bin_kernel(
    brick_ref, count_ref, cell_ref, frac_ref, normal_ref, weight_ref, guess_ref, points_ref, v_ref,
    packed, split, edge, psend, precv, send, recv,
):
    grid = Grid()
    peers = grid.ns * grid.nr
    me = grid.slab * grid.nr + grid.line
    barrier = pltpu.get_barrier_semaphore()
    for colour in range(2):
        grid.clear_outside(v_ref.at[colour], edge.at[colour])

    def peer(i):
        t = lax.rem(me + i, peers)
        return t, (t // grid.nr, lax.rem(t, grid.nr))

    def greet(i, _):
        pl.semaphore_signal(barrier, inc=1, device_id=peer(i)[1], device_id_type=MESH)
        return 0

    lax.fori_loop(1, peers, greet, 0)

    point = iota((CAP, peers), 0)
    live = jnp.concatenate([(point < count_ref[s : s + 1, :]).astype(F32) for s in range(S_PEER)], axis=0)

    def put(r, first, second, mask=None):
        rows = jnp.concatenate([first, second], axis=0).astype(F32)
        packed[pl.ds(r, peers, stride=8), :] = (rows if mask is None else rows * mask).T

    put(0, cell_ref[0], cell_ref[1])
    put(1, frac_ref[0], frac_ref[1])
    for ch in range(3):
        put(2 + ch, normal_ref[0, ch], normal_ref[1, ch], live)
    put(5, weight_ref[0], weight_ref[1], live)
    put(6, *[jnp.broadcast_to(brick_ref[s : s + 1, :], point.shape) for s in range(S_PEER)])
    packed[pl.ds(7, peers, stride=8), :] = jnp.zeros((peers, 128), F32)

    def tile(t):
        return pl.ds(pl.multiple_of(t * 8, 8), 8)

    pl.semaphore_wait(barrier, peers - 1)

    def send_points(i, _):
        t, device = peer(i)
        pltpu.make_async_remote_copy(packed.at[tile(t)], points_ref.at[tile(me)], psend, precv, device, MESH).start()
        return 0

    lax.fori_loop(1, peers, send_points, 0)
    points_ref[tile(me), :] = packed[tile(me), :]
    deinterleave(guess_ref, split)
    for colour in range(2):
        for zp in range(HALF):
            at = (colour * HALF + zp) * Y_DEV * 8
            v_ref[colour, zp + 1, 1:LAST] = split[at : at + Y_DEV * 8, :].reshape(Y_DEV, *TILE)
    halos = [grid.halo(v_ref.at[c], edge.at[c], send.at[c], recv.at[c]) for c in range(2)]
    for colour in range(2):
        grid.start(halos[colour])
    for colour in range(2):
        grid.take(halos[colour])
        rims(v_ref.at[colour], edge.at[colour])
    others = pl.ds(0, (peers - 1) * 8)
    every = pltpu.make_async_remote_copy(packed.at[others], points_ref.at[others], psend, precv, peer(1)[1], MESH)
    every.wait_recv()
    every.wait_send()
    for colour in range(2):
        grid.sent(halos[colour])


def splat_kernel(points_ref, rhs_ref, inv_ref, yface_ref, zface_ref, acc, brick_v, brick_s, f1, f2, sem):
    sources = points_ref.shape[0] // 8
    brick_v[...] = points_ref[pl.ds(6, sources, stride=8), :].astype(I32)
    copy = pltpu.make_async_copy(brick_v, brick_s, sem)
    copy.start()

    def clear(b, _):
        acc[pl.ds(b * 8, 8)] = jnp.zeros((8, 32, 128), F32)
        return 0

    lax.fori_loop(0, Z_DEV * Y_DEV // 8, clear, 0)
    copy.wait()

    lane = iota(TILE, 1)
    left = lane < CAP
    rank = iota(TILE, 0)
    wide_rank = iota((128, 128), 0)

    def group(g, _):
        cell, frac, n0, n1, n2, w, brick = [points_ref[pl.ds(g * 64 + r, 8, stride=8), :] for r in range(7)]
        cell, brick = cell.astype(I32), brick.astype(I32)
        parity, k = cell & 1, cell >> 1
        even = parity == 0
        wl = 0.5 * (0.5 - frac) * (0.5 - frac)
        wm = 0.75 - frac * frac
        wh = 0.5 * (0.5 + frac) * (0.5 + frac)
        beside = jnp.where(even, wh, wl)
        beyond = jnp.where(even, wl, wh)
        k2 = jnp.where(even, k - 1, k + 1)
        zl, yl = brick >> 4, brick & 15
        side = (parity + zl + yl + (zl >> 3)) & 1
        h1 = side * 4 + (k >> 7)
        h2 = (1 - side) * 4 + (k >> 7)
        inside = (k2 >= 0) & (k2 < NX // 2)
        h3 = jnp.where(inside, (1 - side) * 4 + (k2 >> 7), -1)
        none = jnp.full(TILE, -1, I32)
        zero = jnp.zeros(TILE, F32)

        def swap(x):
            return pltpu.roll(x, 64, 1)

        def both(x, y):
            return (jnp.where(left, x, swap(y)), jnp.where(left, swap(x), y))

        lanes_ = both(k & 127, k2 & 127)
        ha, hb = both(h1, h3), both(h2, none)
        wa, wb = both(wm, beyond), both(beside, zero)
        vals = [both(v, v) for v in (n0, n1, n2, w)]
        for r in range(8):
            for s in range(S_PEER):
                def row(x):
                    return x[s][r : r + 1, :]

                unit = jnp.where(rank == row(ha), row(wa), jnp.where(rank == row(hb), row(wb), 0.0))
                a = jnp.concatenate([unit * row(v) for v in vals], axis=0)
                onehot = (wide_rank == row(lanes_)).astype(F32).astype(BF16)
                out = lax.dot_general(
                    jnp.concatenate(parts(a), axis=0), onehot, (((1,), (1,)), ((), ())), preferred_element_type=F32
                )
                b = brick_s[g * 8 + r, s * CAP]
                acc[b] = acc[b] + (out[:32] + out[32:])
        return 0

    lax.fori_loop(0, sources // 8, group, 0)

    low = low_half((Y_DEV, *TILE))

    def fields(zp, ch):
        one = acc[pl.ds(zp * Y_DEV, Y_DEV), ch * 8 : ch * 8 + 8, :]
        two = acc[pl.ds((zp + HALF) * Y_DEV, Y_DEV), ch * 8 : ch * 8 + 8, :]
        return jnp.where(low, one, two), swap_halves(jnp.where(low, two, one))

    nil = jnp.zeros((1, *TILE), F32)
    for colour in range(2):
        for zp in range(HALF):
            f1[colour, zp, 0:1] = nil
            f1[colour, zp, Y_DEV + 1 : Y_DEV + 2] = nil

    def planes(pair, _):
        for odd in range(2):
            zp = pair * 2 + odd
            x = fields(zp, 0)
            y = fields(zp, 1)
            z = fields(zp, 2)
            d = fields(zp, 3)
            for colour in range(2):
                def slope(tiles, parity):
                    other = neighbour(tiles, parity)
                    return tiles - other if parity == 0 else other - tiles

                rhs_ref[colour, zp] = by_rows(x[1 - colour], (odd + colour) % 2, slope)
                f1[colour, zp, 1 : Y_DEV + 1] = y[colour]
                f2[colour, zp + 1] = z[colour]
                inv_ref[colour, zp] = 1.0 / (32.0 + 48.0 * d[colour])
                yface_ref[0, colour, zp] = y[colour][0]
                yface_ref[1, colour, zp] = y[colour][Y_DEV - 1]
        return 0

    lax.fori_loop(0, HALF // 2, planes, 0)
    zface_ref[0] = acc[0:Y_DEV, 16:24, :]
    zface_ref[1] = acc[(Z_DEV - 1) * Y_DEV :, 16:24, :]
    for colour in range(2):
        f2[colour, 0] = swap_halves(jnp.where(low, f2[colour, HALF], 0.0))
        f2[colour, HALF + 1] = swap_halves(jnp.where(low, 0.0, f2[colour, 1]))

    def finish(zp, _):
        for colour in range(2):
            o = 1 - colour
            spread = rhs_ref[colour, zp] + f1[o, zp, 2:] - f1[o, zp, :-2] + f2[o, zp + 2] - f2[o, zp]
            rhs_ref[colour, zp] = -6.0 * spread
        return 0

    lax.fori_loop(0, HALF, finish, 0)


def relax_kernel(rhs_in, inv_ref, start_ref, yface_ref, zface_ref, out_ref, v, edge, rhs, yin, zfin, send, recv, fsend, frecv):
    grid = Grid()
    versions = [start_ref.at[0], start_ref.at[1]] + [v.at[n] for n in range(2 * SWEEPS - 1)]

    def clear(n, _):
        grid.clear_outside(v.at[n], edge.at[n])
        return 0

    lax.fori_loop(0, 2 * SWEEPS - 1, clear, 0)
    for q, d in enumerate(SIDES[:4]):
        s = 0 if d[q < 2] == 1 else 1
        @pl.when(jnp.logical_not(grid.exists((-d[0], -d[1]))))
        def _():
            if d[0] == 0:
                yin[s] = jnp.zeros(yin.shape[1:], F32)
            else:
                zfin[s] = jnp.zeros(zfin.shape[1:], F32)
    grid.greet_neighbours()
    grid.await_neighbours()
    faces = []
    for q, d in enumerate(SIDES[:4]):
        s = 0 if d[q < 2] == 1 else 1
        if d[0] == 0:
            src, dst = yface_ref.at[1 - s], yin.at[s]
        else:
            src, dst = zface_ref.at[1 - s], zfin.at[s]
        faces.append((d, pltpu.make_async_remote_copy(src, dst, fsend.at[q], frecv.at[q], grid.device(d), MESH)))
    grid.start(faces)
    for colour in range(2):
        for zp in range(HALF):
            rhs[colour, zp] = rhs_in[colour, zp]
    low = low_half((Y_DEV, *TILE))
    grid.take(faces)
    for colour in range(2):
        for zp in range(HALF):
            rhs[colour, zp, 0] += 6.0 * yin[0, 1 - colour, zp]
            rhs[colour, zp, Y_DEV - 1] -= 6.0 * yin[1, 1 - colour, zp]
        below, above = zfin[0], zfin[1]
        if colour == 1:
            below, above = swap_halves(below), swap_halves(above)
        rhs[colour, 0] += jnp.where(low, 6.0 * below, 0.0)
        rhs[colour, HALF - 1] -= jnp.where(low, 0.0, 6.0 * above)

    sent = [faces]
    for step in range(2 * SWEEPS):
        same, opp, colour = versions[step], versions[step + 1], step % 2
        new = versions[step + 2] if step < 2 * SWEEPS - 1 else None

        def update(zp, y, count):
            parity = (zp if isinstance(zp, int) else zp[1]) + y + colour
            zp = zp if isinstance(zp, int) else zp[0]
            s1 = same[zp, y : y + count + 2] + same[zp + 2, y : y + count + 2]
            o1 = opp[zp, y : y + count + 2] + opp[zp + 2, y : y + count + 2]
            s0 = same[zp + 1, y : y + count + 2]
            around = s1[1:-1] + s0[:-2] + s0[2:]
            diagonal = s1[:-2] + s1[2:]
            across = 2.0 * around + (o1[:-2] + o1[2:])
            total = rhs[colour, zp, y : y + count] + 2.0 * diagonal + across
            other = neighbour(across, parity % 2) if count == 1 else by_rows(across, parity % 2, neighbour)
            value = (total + other) * inv_ref[colour, zp, y : y + count]
            if new is not None:
                new[zp + 1, y + 1 : y + 1 + count] = value
            if step >= 2 * SWEEPS - 2:
                out_ref[colour, zp, y : y + count] = value

        for zp in range(1, HALF - 1):
            for y in (0, Y_DEV - 1):
                update(zp, y, 1)
        for zp in (0, HALF - 1):
            update(zp, 0, Y_DEV)
        if new is not None:
            pairs = grid.halo(new, edge.at[step], send.at[step], recv.at[step])
            grid.start(pairs)
            sent.append(pairs)

        def inner(pair, _):
            for odd in range(2):
                update((pair * 2 + 1 + odd, 1 + odd), 1, Y_DEV - 2)
            return 0

        lax.fori_loop(0, HALF // 2 - 1, inner, 0)
        if new is not None:
            grid.take(pairs)
            rims(new, edge.at[step])

    for pairs in sent:
        grid.sent(pairs)


def interleave_kernel(in_ref, out_ref):
    col, row = iota((256, 256), 1), iota((256, 256), 0)
    place = (col == jnp.where(row < 128, 2 * row, 2 * row - 255)).astype(BF16)
    rows = Z_DEV * Y_DEV
    cells = iota((rows, 128), 0)
    even = (cells + cells // Y_DEV) % 2 == 0
    for i in range(4):
        colours = []
        for colour in range(2):
            base = [((colour * HALF + z % HALF) * Y_DEV) * 8 + (z // HALF) * 4 + i for z in range(Z_DEV)]
            colours.append(jnp.concatenate([in_ref[pl.ds(b, Y_DEV, stride=8), :] for b in base], axis=0))
        red, black = colours
        both = jnp.concatenate([jnp.where(even, red, black), jnp.where(even, black, red)], axis=1)
        high, low = parts(both)
        merged = jnp.dot(high, place, preferred_element_type=F32) + jnp.dot(low, place, preferred_element_type=F32)
        out_ref[:, :, 256 * i : 256 * (i + 1)] = merged.reshape(Z_DEV, Y_DEV, 256)


VM = pl.BlockSpec(memory_space=pltpu.VMEM)


def call(kernel, outs, scratch, count, limit, **params):
    return pl.pallas_call(
        kernel,
        out_shape=outs,
        in_specs=[VM] * count,
        out_specs=jax.tree.map(lambda _: VM, outs),
        scratch_shapes=scratch,
        compiler_params=pltpu.CompilerParams(vmem_limit_bytes=limit << 20, **params),
    )


def shards(slot_brick, slot_count, point_cell, point_frac, point_normal, point_weight, guess):
    peers = point_cell.shape[1]
    full = jax.ShapeDtypeStruct((2, HALF, Y_DEV, *TILE), F32)
    steps = 2 * SWEEPS - 1

    def last(x):
        return jnp.moveaxis(x[0], 0, -1)

    points, start = call(
        bin_kernel,
        (jax.ShapeDtypeStruct((peers * 8, 128), F32), jax.ShapeDtypeStruct((2, *RIM), F32)),
        [
            pltpu.VMEM((peers * 8, 128), F32),
            pltpu.VMEM((2 * HALF * Y_DEV * 8, 128), F32),
            pltpu.VMEM((2, 2, Y_DEV + 2, *TILE), F32),
            pltpu.SemaphoreType.DMA,
            pltpu.SemaphoreType.DMA,
            pltpu.SemaphoreType.DMA((2, 8)),
            pltpu.SemaphoreType.DMA((2, 8)),
        ],
        7,
        24,
        collective_id=0,
        has_side_effects=True,
    )(last(slot_brick), last(slot_count), last(point_cell), last(point_frac), last(point_normal), last(point_weight), guess)
    outs = (
        full,
        full,
        jax.ShapeDtypeStruct((2, 2, HALF, *TILE), F32),
        jax.ShapeDtypeStruct((2, Y_DEV, *TILE), F32),
    )
    rhs, inv, yface, zface = call(
        splat_kernel,
        outs,
        [
            pltpu.VMEM((Z_DEV * Y_DEV, 32, 128), F32),
            pltpu.VMEM((peers, 128), I32),
            pltpu.SMEM((peers, 128), I32),
            pltpu.VMEM((2, HALF, Y_DEV + 2, *TILE), F32),
            pltpu.VMEM((2, HALF + 2, Y_DEV, *TILE), F32),
            pltpu.SemaphoreType.DMA,
        ],
        1,
        32,
    )(points)
    relaxed = call(
        relax_kernel,
        full,
        [
            pltpu.VMEM((steps, *RIM), F32),
            pltpu.VMEM((steps, 2, Y_DEV + 2, *TILE), F32),
            pltpu.VMEM((2, HALF, Y_DEV, *TILE), F32),
            pltpu.VMEM((2, 2, HALF, *TILE), F32),
            pltpu.VMEM((2, Y_DEV, *TILE), F32),
            pltpu.SemaphoreType.DMA((steps, 8)),
            pltpu.SemaphoreType.DMA((steps, 8)),
            pltpu.SemaphoreType.DMA((4,)),
            pltpu.SemaphoreType.DMA((4,)),
        ],
        5,
        32,
        collective_id=1,
        has_side_effects=True,
    )(rhs, inv, start, yface, zface)
    return call(interleave_kernel, jax.ShapeDtypeStruct((Z_DEV, Y_DEV, NX), F32), [], 1, 16)(relaxed.reshape(-1, 128))


def solution(mesh):
    placed = (
        P(("slab", "row"), None, None),
        P(("slab", "row"), None, None),
        P(("slab", "row"), None, None, None),
        P(("slab", "row"), None, None, None),
        P(("slab", "row"), None, None, None, None),
        P(("slab", "row"), None, None, None),
        P("slab", "row", None),
    )
    return jax.shard_map(
        shards, mesh=mesh, in_specs=placed, out_specs=P("slab", "row", None), check_vma=False
    )
```

```python
import functools

import jax
import jax.numpy as jnp
from jax import lax
from jax.experimental import pallas as pl
from jax.experimental.pallas import tpu as pltpu
from jax.sharding import PartitionSpec as P

Z_DEV = 16
Y_DEV = 16
NX = 1024
CAP = 64
S_PEER = 2
SWEEPS = 3
HALF = Z_DEV // 2
TILE = (8, 128)
MESH = pl.DeviceIdType.MESH
LOGICAL = pl.DeviceIdType.LOGICAL
F32 = jnp.float32
BF16 = jnp.bfloat16
I32 = jnp.int32


def iota(shape, dim):
    return lax.broadcasted_iota(I32, shape, dim)


def swap_halves(tiles):
    return pltpu.roll(tiles, 4, tiles.ndim - 2)


def low_half(shape):
    return iota(shape, len(shape) - 2) < 4


def neighbour(tiles, parity):
    shape = tiles.shape
    lane, sub = iota(shape, len(shape) - 1), iota(shape, len(shape) - 2) % 4
    if parity == 0:
        near = pltpu.roll(tiles, 1, len(shape) - 1)
        far = pltpu.roll(near, 1, len(shape) - 2)
        edge, end = lane == 0, sub == 0
    else:
        near = pltpu.roll(tiles, 127, len(shape) - 1)
        far = pltpu.roll(near, 7, len(shape) - 2)
        edge, end = lane == 127, sub == 3
    return jnp.where(edge, jnp.where(end, 0.0, far), near)


def by_rows(tiles, parity, function):
    pairs = tiles.reshape(tiles.shape[0] // 2, 2, *TILE)
    done = [function(pairs[:, q], (parity + q) % 2) for q in range(2)]
    return jnp.stack(done, axis=1).reshape(tiles.shape)


def parts(x):
    high = x.astype(BF16)
    return high, (x - high.astype(F32)).astype(BF16)


def deinterleave(guess_ref, start_ref):
    col, row = iota((256, 256), 1), iota((256, 256), 0)
    place = (row == jnp.where(col < 128, 2 * col, 2 * col - 255)).astype(BF16)
    rows = Z_DEV * Y_DEV
    cells = iota((rows, 128), 0)
    even = (cells + cells // Y_DEV) % 2 == 0
    for i in range(4):
        chunk = guess_ref[:, :, 256 * i : 256 * (i + 1)].reshape(rows, 256)
        high, low = parts(chunk)
        split = jnp.dot(high, place, preferred_element_type=F32) + jnp.dot(low, place, preferred_element_type=F32)
        first, second = split[:, :128], split[:, 128:]
        colours = (jnp.where(even, first, second), jnp.where(even, second, first))
        for colour in range(2):
            for z in range(Z_DEV):
                base = ((colour * HALF + z % HALF) * Y_DEV) * 8 + (z // HALF) * 4 + i
                start_ref[pl.ds(base, Y_DEV, stride=8), :] = colours[colour][z * Y_DEV : (z + 1) * Y_DEV]


SIDES = [(1, 1), (1, -1), (-1, 1), (-1, -1), (1, 0), (-1, 0), (0, 1), (0, -1)]
FACES = SIDES[4:]
EDGE = (2, HALF + 2, *TILE)
LAST = Y_DEV + 1
RIM = (HALF + 2, Y_DEV + 2, *TILE)


class Grid:
    def __init__(self):
        self.ns, self.nr = lax.axis_size("slab"), lax.axis_size("row")
        self.slab, self.line = lax.axis_index("slab"), lax.axis_index("row")

    def exists(self, d):
        tests = []
        for step, at, size in ((d[0], self.slab, self.ns), (d[1], self.line, self.nr)):
            if step == 1:
                tests.append(at < size - 1)
            if step == -1:
                tests.append(at > 0)
        return tests[0] if len(tests) == 1 else tests[0] & tests[1]

    def device(self, d):
        return (self.slab + d[0], self.line + d[1])

    def greet_neighbours(self):
        barrier = pltpu.get_barrier_semaphore()
        for d in SIDES:
            @pl.when(self.exists(d))
            def _():
                pl.semaphore_signal(barrier, inc=1, device_id=self.device(d), device_id_type=MESH)

    def await_neighbours(self):
        counts = [
            1 + (at > 0).astype(I32) + (at < size - 1).astype(I32)
            for at, size in ((self.slab, self.ns), (self.line, self.nr))
        ]
        pl.semaphore_wait(pltpu.get_barrier_semaphore(), counts[0] * counts[1] - 1)

    def start(self, pairs):
        for d, copy in pairs:
            @pl.when(self.exists(d))
            def _():
                copy.start()

    def take(self, pairs):
        for d, copy in pairs:
            @pl.when(self.exists((-d[0], -d[1])))
            def _():
                copy.wait_recv()

    def sent(self, pairs):
        for d, copy in pairs:
            @pl.when(self.exists(d))
            def _():
                copy.wait_send()

    def clear_outside(self, tiles, edge):
        for d in SIDES:
            @pl.when(jnp.logical_not(self.exists((-d[0], -d[1]))))
            def _():
                if d[0] == 0:
                    y = 0 if d[1] == 1 else LAST
                    tiles[1 : HALF + 1, y : y + 1] = jnp.zeros((HALF, 1, *TILE), F32)
                else:
                    at, size = EDGE_AT[d[1]]
                    edge[0 if d[0] == 1 else 1, at : at + size] = jnp.zeros((size, *TILE), F32)

    def halo(self, tiles, edge, face, send, recv):
        pairs = []
        for q, d in enumerate(SIDES):
            at, size = EDGE_AT[d[1]]
            side = 0 if d[0] == 1 else 1
            if d[0] == 0:
                src, dst = (tiles.at[pl.ds(1, HALF), pl.ds(y, 1)] for y in ((Y_DEV, 0) if d[1] == 1 else (1, LAST)))
            elif d[1] == 0:
                src, dst = face.at[side], edge.at[side, pl.ds(at, size)]
            else:
                src = tiles.at[HALF if d[0] == 1 else 1, pl.ds(Y_DEV if d[1] == 1 else 1, 1)]
                dst = edge.at[side, pl.ds(at, size)]
            pairs.append((d, pltpu.make_async_remote_copy(src, dst, send.at[q], recv.at[q], self.device(d), MESH)))
        return pairs


EDGE_AT = {0: (0, HALF), 1: (HALF, 1), -1: (HALF + 1, 1)}


def pack_faces(tiles, face):
    low = low_half((HALF, *TILE))
    face[0] = jnp.where(low, swap_halves(tiles[HALF, 1 : HALF + 1]), tiles[HALF, HALF + 1 : LAST])
    face[1] = jnp.where(low, tiles[1, 1 : HALF + 1], swap_halves(tiles[1, HALF + 1 : LAST]))


def rims(tiles, edge):
    low = low_half((HALF, *TILE))
    top, bottom = tiles[HALF], tiles[1]
    below, above = edge[0], edge[1]
    first, second = slice(1, HALF + 1), slice(HALF + 1, LAST)
    tiles[0, first] = jnp.where(low, below[:HALF], swap_halves(top[first]))
    tiles[0, second] = swap_halves(jnp.where(low, top[second], below[:HALF]))
    tiles[HALF + 1, first] = swap_halves(jnp.where(low, above[:HALF], bottom[first]))
    tiles[HALF + 1, second] = jnp.where(low, swap_halves(bottom[second]), above[:HALF])
    for y, at in ((slice(0, 1), HALF), (slice(LAST, LAST + 1), HALF + 1)):
        tiles[0, y] = swap_halves(jnp.where(low[:1], top[y], below[at : at + 1]))
        tiles[HALF + 1, y] = swap_halves(jnp.where(low[:1], above[at : at + 1], bottom[y]))


def bin_kernel(
    brick_in, count_in, cell_in, frac_in, normal_in, weight_in, guess_in, points_ref, v_ref,
    brick_ref, count_ref, cell_ref, frac_ref, normal_ref, weight_ref, guess_ref,
    packed, split, edge, face, load, psend, precv, send, recv,
):
    loads = [
        pltpu.make_async_copy(src, dst, load.at[q])
        for q, (src, dst) in enumerate(
            (
                (guess_in, guess_ref), (brick_in, brick_ref), (count_in, count_ref), (cell_in, cell_ref),
                (frac_in, frac_ref), (normal_in, normal_ref), (weight_in, weight_ref),
            )
        )
    ]
    for copy in loads:
        copy.start()
    grid = Grid()
    peers = grid.ns * grid.nr
    me = grid.slab * grid.nr + grid.line
    barrier = pltpu.get_barrier_semaphore()
    for colour in range(2):
        grid.clear_outside(v_ref.at[colour], edge.at[colour])

    def peer(i):
        return lax.rem(me + lax.rem(i + peers // 2 - 1, peers - 1) + 1, peers)

    def greet(i, _):
        pl.semaphore_signal(barrier, inc=1, device_id=peer(i), device_id_type=LOGICAL)
        return 0

    lax.fori_loop(0, peers - 1, greet, 0)

    loads[0].wait()
    deinterleave(guess_ref, split)
    for colour in range(2):
        for zp in range(HALF):
            at = (colour * HALF + zp) * Y_DEV * 8
            v_ref[colour, zp + 1, 1:LAST] = split[at : at + Y_DEV * 8, :].reshape(Y_DEV, *TILE)
        pack_faces(v_ref.at[colour], face.at[colour])
    for copy in loads[1:]:
        copy.wait()

    point = iota((CAP, peers), 0)
    live = jnp.concatenate([(point < count_ref[s : s + 1, :]).astype(F32) for s in range(S_PEER)], axis=0)

    def put(r, first, second, mask=None):
        rows = jnp.concatenate([first, second], axis=0).astype(F32)
        packed[pl.ds(r, peers, stride=8), :] = (rows if mask is None else rows * mask).T

    put(0, cell_ref[0], cell_ref[1])
    put(1, frac_ref[0], frac_ref[1])
    for ch in range(3):
        put(2 + ch, normal_ref[0, ch], normal_ref[1, ch], live)
    put(5, weight_ref[0], weight_ref[1], live)
    put(6, *[jnp.broadcast_to(brick_ref[s : s + 1, :], point.shape) for s in range(S_PEER)])
    packed[pl.ds(7, peers, stride=8), :] = jnp.zeros((peers, 128), F32)

    def tile(t):
        return pl.ds(pl.multiple_of(t * 8, 8), 8)

    pl.semaphore_wait(barrier, peers - 1)

    def send_points(i, _):
        t = peer(i)
        pltpu.make_async_remote_copy(packed.at[tile(t)], points_ref.at[tile(me)], psend, precv, t, LOGICAL).start()
        return 0

    lax.fori_loop(0, peers - 1, send_points, 0)
    halos = [grid.halo(v_ref.at[c], edge.at[c], face.at[c], send.at[c], recv.at[c]) for c in range(2)]
    for colour in range(2):
        grid.start(halos[colour])
    points_ref[tile(me), :] = packed[tile(me), :]
    for colour in range(2):
        grid.take(halos[colour])
        rims(v_ref.at[colour], edge.at[colour])
    others = pl.ds(0, (peers - 1) * 8)
    every = pltpu.make_async_remote_copy(packed.at[others], points_ref.at[others], psend, precv, peer(0), LOGICAL)
    every.wait_recv()
    every.wait_send()
    for colour in range(2):
        grid.sent(halos[colour])


def splat_kernel(points_ref, rhs_ref, inv_ref, yface_ref, zface_ref, acc, brick_v, brick_s, f1, f2, sem):
    sources = points_ref.shape[0] // 8
    brick_v[...] = points_ref[pl.ds(6, sources, stride=8), :].astype(I32)
    copy = pltpu.make_async_copy(brick_v, brick_s, sem)
    copy.start()

    def clear(b, _):
        acc[pl.ds(b * 8, 8)] = jnp.zeros((8, 32, 128), F32)
        return 0

    lax.fori_loop(0, Z_DEV * Y_DEV // 8, clear, 0)
    copy.wait()

    lane = iota(TILE, 1)
    left = lane < CAP
    rank = iota(TILE, 0)
    wide_rank = iota((128, 128), 0)

    def group(g, _):
        cell, frac, n0, n1, n2, w, brick = [points_ref[pl.ds(g * 64 + r, 8, stride=8), :] for r in range(7)]
        cell, brick = cell.astype(I32), brick.astype(I32)
        parity, k = cell & 1, cell >> 1
        even = parity == 0
        wl = 0.5 * (0.5 - frac) * (0.5 - frac)
        wm = 0.75 - frac * frac
        wh = 0.5 * (0.5 + frac) * (0.5 + frac)
        beside = jnp.where(even, wh, wl)
        beyond = jnp.where(even, wl, wh)
        k2 = jnp.where(even, k - 1, k + 1)
        zl, yl = brick >> 4, brick & 15
        side = (parity + zl + yl + (zl >> 3)) & 1
        h1 = side * 4 + (k >> 7)
        h2 = (1 - side) * 4 + (k >> 7)
        inside = (k2 >= 0) & (k2 < NX // 2)
        h3 = jnp.where(inside, (1 - side) * 4 + (k2 >> 7), -1)
        none = jnp.full(TILE, -1, I32)
        zero = jnp.zeros(TILE, F32)

        def swap(x):
            return pltpu.roll(x, 64, 1)

        def both(x, y):
            return (jnp.where(left, x, swap(y)), jnp.where(left, swap(x), y))

        lanes_ = both(k & 127, k2 & 127)
        ha, hb = both(h1, h3), both(h2, none)
        wa, wb = both(wm, beyond), both(beside, zero)
        vals = [both(v, v) for v in (n0, n1, n2, w)]
        for r in range(8):
            weights, onehots = [], []
            for s in range(S_PEER):
                def row(x):
                    return x[s][r : r + 1, :]

                unit = jnp.where(rank == row(ha), row(wa), jnp.where(rank == row(hb), row(wb), 0.0))
                weights.append(jnp.concatenate(parts(jnp.concatenate([unit * row(v) for v in vals], axis=0)), axis=0))
                onehots.append((wide_rank == row(lanes_)).astype(F32).astype(BF16))
            apart = jnp.zeros(weights[0].shape, BF16)
            diagonal = jnp.concatenate(
                [jnp.concatenate([weights[0], apart], axis=1), jnp.concatenate([apart, weights[1]], axis=1)], axis=0
            )
            out = lax.dot_general(
                diagonal, jnp.concatenate(onehots, axis=1), (((1,), (1,)), ((), ())), preferred_element_type=F32
            )
            for s in range(S_PEER):
                b = brick_s[g * 8 + r, s * CAP]
                acc[b] = acc[b] + (out[s * 64 : s * 64 + 32] + out[s * 64 + 32 : s * 64 + 64])
        return 0

    lax.fori_loop(0, sources // 8, group, 0)

    low = low_half((Y_DEV, *TILE))

    def fields(zp, ch):
        one = acc[pl.ds(zp * Y_DEV, Y_DEV), ch * 8 : ch * 8 + 8, :]
        two = acc[pl.ds((zp + HALF) * Y_DEV, Y_DEV), ch * 8 : ch * 8 + 8, :]
        return jnp.where(low, one, two), swap_halves(jnp.where(low, two, one))

    nil = jnp.zeros((1, *TILE), F32)
    for colour in range(2):
        for zp in range(HALF):
            f1[colour, zp, 0:1] = nil
            f1[colour, zp, Y_DEV + 1 : Y_DEV + 2] = nil

    def planes(pair, _):
        for odd in range(2):
            zp = pair * 2 + odd
            x = fields(zp, 0)
            y = fields(zp, 1)
            z = fields(zp, 2)
            d = fields(zp, 3)
            for colour in range(2):
                def slope(tiles, parity):
                    other = neighbour(tiles, parity)
                    return tiles - other if parity == 0 else other - tiles

                rhs_ref[colour, zp] = by_rows(x[1 - colour], (odd + colour) % 2, slope)
                f1[colour, zp, 1 : Y_DEV + 1] = y[colour]
                f2[colour, zp + 1] = z[colour]
                inv_ref[colour, zp] = 1.0 / (32.0 + 48.0 * d[colour])
                yface_ref[0, colour, zp] = y[colour][0]
                yface_ref[1, colour, zp] = y[colour][Y_DEV - 1]
        return 0

    lax.fori_loop(0, HALF // 2, planes, 0)
    zface_ref[0] = acc[0:Y_DEV, 16:24, :]
    zface_ref[1] = acc[(Z_DEV - 1) * Y_DEV :, 16:24, :]
    for colour in range(2):
        f2[colour, 0] = swap_halves(jnp.where(low, f2[colour, HALF], 0.0))
        f2[colour, HALF + 1] = swap_halves(jnp.where(low, 0.0, f2[colour, 1]))

    def finish(zp, _):
        for colour in range(2):
            o = 1 - colour
            spread = rhs_ref[colour, zp] + f1[o, zp, 2:] - f1[o, zp, :-2] + f2[o, zp + 2] - f2[o, zp]
            rhs_ref[colour, zp] = -6.0 * spread
        return 0

    lax.fori_loop(0, HALF, finish, 0)


def relax_kernel(rhs_in, inv_ref, start_ref, yface_ref, zface_ref, out_ref, v, edge, rhs, yin, zfin, face, send, recv, fsend, frecv):
    grid = Grid()
    versions = [start_ref.at[0], start_ref.at[1]] + [v.at[n] for n in range(2 * SWEEPS - 1)]

    def clear(n, _):
        grid.clear_outside(v.at[n], edge.at[n])
        return 0

    grid.greet_neighbours()
    lax.fori_loop(0, 2 * SWEEPS - 1, clear, 0)
    for d in FACES:
        s = 0 if sum(d) == 1 else 1

        @pl.when(jnp.logical_not(grid.exists((-d[0], -d[1]))))
        def _():
            if d[0] == 0:
                yin[s] = jnp.zeros(yin.shape[1:], F32)
            else:
                zfin[s] = jnp.zeros(zfin.shape[1:], F32)

    def update(step, zp, y, count):
        zp, parity = (zp, zp) if isinstance(zp, int) else zp
        same, opp, colour = versions[step], versions[step + 1], step % 2
        outer = count == 1 or (isinstance(zp, int) and zp in (0, HALF - 1))
        right = (rhs if outer else rhs_in)[colour, zp, y : y + count]
        parity = (parity + y + colour) % 2
        s1 = same[zp, y : y + count + 2] + same[zp + 2, y : y + count + 2]
        o1 = opp[zp, y : y + count + 2] + opp[zp + 2, y : y + count + 2]
        s0 = same[zp + 1, y : y + count + 2]
        around = s1[1:-1] + s0[:-2] + s0[2:]
        diagonal = s1[:-2] + s1[2:]
        across = 2.0 * around + (o1[:-2] + o1[2:])
        total = right + 2.0 * diagonal + across
        other = neighbour(across, parity) if count == 1 else by_rows(across, parity, neighbour)
        value = (total + other) * inv_ref[colour, zp, y : y + count]
        if step < 2 * SWEEPS - 1:
            versions[step + 2][zp + 1, y + 1 : y + 1 + count] = value
        if step >= 2 * SWEEPS - 2:
            out_ref[colour, zp, y : y + count] = value

    def inner(step):
        def planes(pair, _):
            for odd in range(2):
                update(step, (pair * 2 + 1 + odd, 1 + odd), 1, Y_DEV - 2)
            return 0

        lax.fori_loop(0, HALF // 2 - 1, planes, 0)

    def outer(step):
        for zp in (0, HALF - 1):
            update(step, zp, 0, Y_DEV)
        for zp in range(1, HALF - 1):
            for y in (0, Y_DEV - 1):
                update(step, zp, y, 1)

    faces = []
    for q, d in enumerate(FACES):
        s = 0 if sum(d) == 1 else 1
        src, dst = (yface_ref, yin) if d[0] == 0 else (zface_ref, zfin)
        faces.append(
            (d, pltpu.make_async_remote_copy(src.at[1 - s], dst.at[s], fsend.at[q], frecv.at[q], grid.device(d), MESH))
        )
    inner(0)
    grid.await_neighbours()
    grid.start(faces)
    low = low_half((Y_DEV, *TILE))
    for colour in range(2):
        for zp in (0, HALF - 1):
            rhs[colour, zp] = rhs_in[colour, zp]
        for zp in range(1, HALF - 1):
            for y in (0, Y_DEV - 1):
                rhs[colour, zp, y] = rhs_in[colour, zp, y]
    grid.take(faces)
    for colour in range(2):
        for zp in range(HALF):
            rhs[colour, zp, 0] += 6.0 * yin[0, 1 - colour, zp]
            rhs[colour, zp, Y_DEV - 1] -= 6.0 * yin[1, 1 - colour, zp]
        below, above = zfin[0], zfin[1]
        if colour == 1:
            below, above = swap_halves(below), swap_halves(above)
        rhs[colour, 0] += jnp.where(low, 6.0 * below, 0.0)
        rhs[colour, HALF - 1] -= jnp.where(low, 0.0, 6.0 * above)

    sent = [faces]
    for step in range(2 * SWEEPS):
        outer(step)
        if step < 2 * SWEEPS - 1:
            new = versions[step + 2]
            pack_faces(new, face.at[step])
            pairs = grid.halo(new, edge.at[step], face.at[step], send.at[step], recv.at[step])
            grid.start(pairs)
            sent.append(pairs)
        if step > 0:
            inner(step)
        if step < 2 * SWEEPS - 1:
            grid.take(pairs)
            rims(new, edge.at[step])

    for pairs in sent:
        grid.sent(pairs)


def interleave_kernel(in_ref, out_ref):
    col, row = iota((256, 256), 1), iota((256, 256), 0)
    place = (col == jnp.where(row < 128, 2 * row, 2 * row - 255)).astype(BF16)
    rows = Z_DEV * Y_DEV
    cells = iota((rows, 128), 0)
    even = (cells + cells // Y_DEV) % 2 == 0
    for i in range(4):
        colours = []
        for colour in range(2):
            base = [((colour * HALF + z % HALF) * Y_DEV) * 8 + (z // HALF) * 4 + i for z in range(Z_DEV)]
            colours.append(jnp.concatenate([in_ref[pl.ds(b, Y_DEV, stride=8), :] for b in base], axis=0))
        red, black = colours
        both = jnp.concatenate([jnp.where(even, red, black), jnp.where(even, black, red)], axis=1)
        high, low = parts(both)
        merged = jnp.dot(high, place, preferred_element_type=F32) + jnp.dot(low, place, preferred_element_type=F32)
        out_ref[:, :, 256 * i : 256 * (i + 1)] = merged.reshape(Z_DEV, Y_DEV, 256)


VM = pl.BlockSpec(memory_space=pltpu.VMEM)


def call(kernel, outs, scratch, specs, limit, **params):
    return pl.pallas_call(
        kernel,
        out_shape=outs,
        in_specs=specs,
        out_specs=jax.tree.map(lambda _: VM, outs),
        scratch_shapes=scratch,
        compiler_params=pltpu.CompilerParams(vmem_limit_bytes=limit << 20, **params),
    )


def shards(slot_brick, slot_count, point_cell, point_frac, point_normal, point_weight, guess):
    peers = point_cell.shape[1]
    full = jax.ShapeDtypeStruct((2, HALF, Y_DEV, *TILE), F32)
    steps = 2 * SWEEPS - 1

    def last(x):
        return jnp.moveaxis(x[0], 0, -1)

    args = (last(slot_brick), last(slot_count), last(point_cell), last(point_frac), last(point_normal), last(point_weight), guess)
    points, start = call(
        bin_kernel,
        (jax.ShapeDtypeStruct((peers * 8, 128), F32), jax.ShapeDtypeStruct((2, *RIM), F32)),
        [pltpu.VMEM(a.shape, a.dtype) for a in args]
        + [
            pltpu.VMEM((peers * 8, 128), F32),
            pltpu.VMEM((2 * HALF * Y_DEV * 8, 128), F32),
            pltpu.VMEM((2, *EDGE), F32),
            pltpu.VMEM((2, 2, HALF, *TILE), F32),
            pltpu.SemaphoreType.DMA((7,)),
            pltpu.SemaphoreType.DMA,
            pltpu.SemaphoreType.DMA,
            pltpu.SemaphoreType.DMA((2, 8)),
            pltpu.SemaphoreType.DMA((2, 8)),
        ],
        [pl.BlockSpec(memory_space=pltpu.HBM)] * 7,
        24,
        collective_id=0,
        has_side_effects=True,
    )(*[pltpu.with_memory_space_constraint(a, pltpu.HBM) for a in args])
    outs = (
        full,
        full,
        jax.ShapeDtypeStruct((2, 2, HALF, *TILE), F32),
        jax.ShapeDtypeStruct((2, Y_DEV, *TILE), F32),
    )
    rhs, inv, yface, zface = call(
        splat_kernel,
        outs,
        [
            pltpu.VMEM((Z_DEV * Y_DEV, 32, 128), F32),
            pltpu.VMEM((peers, 128), I32),
            pltpu.SMEM((peers, 128), I32),
            pltpu.VMEM((2, HALF, Y_DEV + 2, *TILE), F32),
            pltpu.VMEM((2, HALF + 2, Y_DEV, *TILE), F32),
            pltpu.SemaphoreType.DMA,
        ],
        [VM],
        32,
    )(points)
    relaxed = call(
        relax_kernel,
        full,
        [
            pltpu.VMEM((steps, *RIM), F32),
            pltpu.VMEM((steps, *EDGE), F32),
            pltpu.VMEM((2, HALF, Y_DEV, *TILE), F32),
            pltpu.VMEM((2, 2, HALF, *TILE), F32),
            pltpu.VMEM((2, Y_DEV, *TILE), F32),
            pltpu.VMEM((steps, 2, HALF, *TILE), F32),
            pltpu.SemaphoreType.DMA((steps, 8)),
            pltpu.SemaphoreType.DMA((steps, 8)),
            pltpu.SemaphoreType.DMA((4,)),
            pltpu.SemaphoreType.DMA((4,)),
        ],
        [VM] * 5,
        32,
        collective_id=1,
        has_side_effects=True,
    )(rhs, inv, start, yface, zface)
    return call(interleave_kernel, jax.ShapeDtypeStruct((Z_DEV, Y_DEV, NX), F32), [], [VM], 16)(relaxed.reshape(-1, 128))


def solution(mesh):
    placed = (
        P(("slab", "row"), None, None),
        P(("slab", "row"), None, None),
        P(("slab", "row"), None, None, None),
        P(("slab", "row"), None, None, None),
        P(("slab", "row"), None, None, None, None),
        P(("slab", "row"), None, None, None),
        P("slab", "row", None),
    )
    return jax.shard_map(
        shards, mesh=mesh, in_specs=placed, out_specs=P("slab", "row", None), check_vma=False
    )
```

```python
import functools

import jax
import jax.numpy as jnp
from jax import lax
from jax.experimental import pallas as pl
from jax.experimental.pallas import tpu as pltpu
from jax.sharding import PartitionSpec as P

Z_DEV = 16
Y_DEV = 16
NX = 1024
CAP = 64
S_PEER = 2
SWEEPS = 3
HALF = Z_DEV // 2
TILE = (8, 128)
MESH = pl.DeviceIdType.MESH
LOGICAL = pl.DeviceIdType.LOGICAL
F32 = jnp.float32
BF16 = jnp.bfloat16
I32 = jnp.int32


def iota(shape, dim):
    return lax.broadcasted_iota(I32, shape, dim)


def swap_halves(tiles):
    return pltpu.roll(tiles, 4, tiles.ndim - 2)


def low_half(shape):
    return iota(shape, len(shape) - 2) < 4


def neighbour(tiles, parity):
    shape = tiles.shape
    lane, sub = iota(shape, len(shape) - 1), iota(shape, len(shape) - 2) % 4
    if parity == 0:
        near = pltpu.roll(tiles, 1, len(shape) - 1)
        far = pltpu.roll(near, 1, len(shape) - 2)
        edge, end = lane == 0, sub == 0
    else:
        near = pltpu.roll(tiles, 127, len(shape) - 1)
        far = pltpu.roll(near, 7, len(shape) - 2)
        edge, end = lane == 127, sub == 3
    return jnp.where(edge, jnp.where(end, 0.0, far), near)


def by_rows(tiles, parity, function):
    pairs = tiles.reshape(tiles.shape[0] // 2, 2, *TILE)
    done = [function(pairs[:, q], (parity + q) % 2) for q in range(2)]
    return jnp.stack(done, axis=1).reshape(tiles.shape)


def parts(x):
    high = x.astype(BF16)
    return high, (x - high.astype(F32)).astype(BF16)


def deinterleave(guess_ref, start_ref):
    col, row = iota((256, 256), 1), iota((256, 256), 0)
    place = (row == jnp.where(col < 128, 2 * col, 2 * col - 255)).astype(BF16)
    rows = Z_DEV * Y_DEV
    cells = iota((rows, 128), 0)
    even = (cells + cells // Y_DEV) % 2 == 0
    for i in range(4):
        chunk = guess_ref[:, :, 256 * i : 256 * (i + 1)].reshape(rows, 256)
        high, low = parts(chunk)
        split = jnp.dot(high, place, preferred_element_type=F32) + jnp.dot(low, place, preferred_element_type=F32)
        first, second = split[:, :128], split[:, 128:]
        colours = (jnp.where(even, first, second), jnp.where(even, second, first))
        for colour in range(2):
            for z in range(Z_DEV):
                base = ((colour * HALF + z % HALF) * Y_DEV) * 8 + (z // HALF) * 4 + i
                start_ref[pl.ds(base, Y_DEV, stride=8), :] = colours[colour][z * Y_DEV : (z + 1) * Y_DEV]


SIDES = [(1, 1), (1, -1), (-1, 1), (-1, -1), (1, 0), (-1, 0), (0, 1), (0, -1)]
WIDE = 2
FULL = (HALF, Y_DEV, *TILE)


def rimmed(width):
    return (HALF + 2 * width, Y_DEV + 2 * width, *TILE)


def edge_shape(width):
    return (2, width, HALF + 2 * width, *TILE)


class Grid:
    def __init__(self):
        self.ns, self.nr = lax.axis_size("slab"), lax.axis_size("row")
        self.slab, self.line = lax.axis_index("slab"), lax.axis_index("row")

    def exists(self, d):
        tests = []
        for step, at, size in ((d[0], self.slab, self.ns), (d[1], self.line, self.nr)):
            if step == 1:
                tests.append(at < size - 1)
            if step == -1:
                tests.append(at > 0)
        return tests[0] if len(tests) == 1 else tests[0] & tests[1]

    def device(self, d):
        return (self.slab + d[0], self.line + d[1])

    def greet_neighbours(self):
        barrier = pltpu.get_barrier_semaphore()
        for d in SIDES:
            @pl.when(self.exists(d))
            def _():
                pl.semaphore_signal(barrier, inc=1, device_id=self.device(d), device_id_type=MESH)

    def await_neighbours(self):
        counts = [
            1 + (at > 0).astype(I32) + (at < size - 1).astype(I32)
            for at, size in ((self.slab, self.ns), (self.line, self.nr))
        ]
        pl.semaphore_wait(pltpu.get_barrier_semaphore(), counts[0] * counts[1] - 1)

    def start(self, pairs):
        for d, copy in pairs:
            @pl.when(self.exists(d))
            def _():
                copy.start()

    def take(self, pairs):
        for d, copy in pairs:
            @pl.when(self.exists((-d[0], -d[1])))
            def _():
                copy.wait_recv()

    def sent(self, pairs):
        for d, copy in pairs:
            @pl.when(self.exists(d))
            def _():
                copy.wait_send()

    def clear(self, pairs):
        for d, dst in pairs:
            @pl.when(jnp.logical_not(self.exists((-d[0], -d[1]))))
            def _():
                dst[...] = jnp.zeros(dst.shape, F32)

    def halo(self, tiles, edge, face, beside=None):
        w = WIDE
        ends = {1: pl.ds(Y_DEV, w), -1: pl.ds(w, w)}
        plan = []
        for d in SIDES:
            side = 0 if d[0] == 1 else 1
            if d[0] == 0:
                dst = tiles.at[pl.ds(w, HALF), pl.ds(0 if d[1] == 1 else Y_DEV + w, w)]
                if beside is not None:
                    dst = beside.at[0 if d[1] == 1 else 1]
                plan.append((d, tiles.at[pl.ds(w, HALF), ends[d[1]]], dst))
            elif d[1] == 0:
                plan.append((d, face.at[side], edge.at[side, pl.ds(0, w), pl.ds(0, HALF)]))
            else:
                dst = edge.at[side, pl.ds(0, w), pl.ds(HALF if d[1] == 1 else HALF + w, w)]
                plan.append((d, tiles.at[pl.ds(HALF if d[0] == 1 else w, w), ends[d[1]]], dst))
        return plan

    def copies(self, plan, send, recv):
        return [
            (d, pltpu.make_async_remote_copy(src, dst, send.at[q], recv.at[q], self.device(d), MESH))
            for q, (d, src, dst) in enumerate(plan)
        ]


def landing(plan):
    return [(d, dst) for d, _, dst in plan]


def pack_top(first, second):
    return jnp.where(low_half(first.shape), swap_halves(first), second)


def pack_bottom(first, second):
    return jnp.where(low_half(first.shape), first, swap_halves(second))


def pack_faces(tiles, face):
    w, half = WIDE, WIDE + HALF
    for p in range(w):
        face[0, p] = pack_top(tiles[HALF + p, w:half], tiles[HALF + p, half : half + HALF])
        face[1, p] = pack_bottom(tiles[w + p, w:half], tiles[w + p, half : half + HALF])


def under(own, corner):
    return swap_halves(jnp.where(low_half(own.shape), own, corner))


def over(own, corner):
    return swap_halves(jnp.where(low_half(own.shape), corner, own))


def rim_planes(tiles, w, p, below, above):
    half = w + HALF
    first, second = slice(w, half), slice(half, half + HALF)
    top, bottom = tiles[HALF + p], tiles[w + p]
    low = low_half((HALF, *TILE))
    up, down = p, HALF + w + p
    tiles[up, first] = jnp.where(low, below[:HALF], swap_halves(top[first]))
    tiles[up, second] = swap_halves(jnp.where(low, top[second], below[:HALF]))
    tiles[down, first] = swap_halves(jnp.where(low, above[:HALF], bottom[first]))
    tiles[down, second] = jnp.where(low, swap_halves(bottom[second]), above[:HALF])
    for y, at in ((slice(0, w), slice(HALF, half)), (slice(Y_DEV + w, Y_DEV + 2 * w), slice(half, half + w))):
        tiles[up, y] = under(top[y], below[at])
        tiles[down, y] = over(bottom[y], above[at])


def rims(tiles, edge):
    for p in range(WIDE):
        rim_planes(tiles, WIDE, p, edge[0, p], edge[1, p])


def bin_kernel(
    brick_in, count_in, cell_in, frac_in, normal_in, weight_in, guess_in, points_ref, v_ref,
    brick_ref, count_ref, cell_ref, frac_ref, normal_ref, weight_ref, guess_ref,
    packed, split, edge, face, load, psend, precv, send, recv,
):
    loads = [
        pltpu.make_async_copy(src, dst, load.at[q])
        for q, (src, dst) in enumerate(
            (
                (guess_in, guess_ref), (brick_in, brick_ref), (count_in, count_ref), (cell_in, cell_ref),
                (frac_in, frac_ref), (normal_in, normal_ref), (weight_in, weight_ref),
            )
        )
    ]
    for copy in loads:
        copy.start()
    grid = Grid()
    peers = grid.ns * grid.nr
    me = grid.slab * grid.nr + grid.line
    barrier = pltpu.get_barrier_semaphore()
    plans = [grid.halo(v_ref.at[c], edge.at[c], face.at[c]) for c in range(2)]
    for plan in plans:
        grid.clear(landing(plan))

    def peer(i):
        return lax.rem(me + i + 1, peers)

    def greet(i, _):
        pl.semaphore_signal(barrier, inc=1, device_id=peer(i), device_id_type=LOGICAL)
        return 0

    lax.fori_loop(0, peers - 1, greet, 0)

    loads[0].wait()
    deinterleave(guess_ref, split)
    for colour in range(2):
        for zp in range(HALF):
            at = (colour * HALF + zp) * Y_DEV * 8
            v_ref[colour, zp + WIDE, WIDE : WIDE + Y_DEV] = split[at : at + Y_DEV * 8, :].reshape(Y_DEV, *TILE)
        pack_faces(v_ref.at[colour], face.at[colour])
    for copy in loads[1:]:
        copy.wait()

    point = iota((CAP, peers), 0)
    live = jnp.concatenate([(point < count_ref[s : s + 1, :]).astype(F32) for s in range(S_PEER)], axis=0)

    def put(r, first, second, mask=None):
        rows = jnp.concatenate([first, second], axis=0).astype(F32)
        packed[pl.ds(r, peers, stride=8), :] = (rows if mask is None else rows * mask).T

    put(0, cell_ref[0], cell_ref[1])
    put(1, frac_ref[0], frac_ref[1])
    for ch in range(3):
        put(2 + ch, normal_ref[0, ch], normal_ref[1, ch], live)
    put(5, weight_ref[0], weight_ref[1], live)
    put(6, *[jnp.broadcast_to(brick_ref[s : s + 1, :], point.shape) for s in range(S_PEER)])
    packed[pl.ds(7, peers, stride=8), :] = jnp.zeros((peers, 128), F32)

    def tile(t):
        return pl.ds(pl.multiple_of(t * 8, 8), 8)

    pl.semaphore_wait(barrier, peers - 1)

    def send_points(i, _):
        t = peer(i)
        pltpu.make_async_remote_copy(packed.at[tile(t)], points_ref.at[tile(me)], psend, precv, t, LOGICAL).start()
        return 0

    lax.fori_loop(0, peers - 1, send_points, 0)
    halos = [grid.copies(plans[c], send.at[c], recv.at[c]) for c in range(2)]
    for colour in range(2):
        grid.start(halos[colour])
    points_ref[tile(me), :] = packed[tile(me), :]
    for colour in range(2):
        grid.take(halos[colour])
        rims(v_ref.at[colour], edge.at[colour])
    others = pl.ds(0, (peers - 1) * 8)
    every = pltpu.make_async_remote_copy(packed.at[others], points_ref.at[others], psend, precv, peer(0), LOGICAL)
    every.wait_recv()
    every.wait_send()
    for colour in range(2):
        grid.sent(halos[colour])


def splat_kernel(points_ref, rhs_ref, inv_ref, ysend_ref, zsend_ref, csend_ref, acc, brick_v, brick_s, f1, f2, sem):
    sources = points_ref.shape[0] // 8
    brick_v[...] = points_ref[pl.ds(6, sources, stride=8), :].astype(I32)
    copy = pltpu.make_async_copy(brick_v, brick_s, sem)
    copy.start()

    def clear(b, _):
        acc[pl.ds(b * 8, 8)] = jnp.zeros((8, 32, 128), F32)
        return 0

    lax.fori_loop(0, Z_DEV * Y_DEV // 8, clear, 0)
    copy.wait()

    lane = iota(TILE, 1)
    left = lane < CAP
    rank = iota(TILE, 0)
    wide_rank = iota((128, 128), 0)

    def group(g, _):
        cell, frac, n0, n1, n2, w, brick = [points_ref[pl.ds(g * 64 + r, 8, stride=8), :] for r in range(7)]
        cell, brick = cell.astype(I32), brick.astype(I32)
        parity, k = cell & 1, cell >> 1
        even = parity == 0
        wl = 0.5 * (0.5 - frac) * (0.5 - frac)
        wm = 0.75 - frac * frac
        wh = 0.5 * (0.5 + frac) * (0.5 + frac)
        beside = jnp.where(even, wh, wl)
        beyond = jnp.where(even, wl, wh)
        k2 = jnp.where(even, k - 1, k + 1)
        zl, yl = brick >> 4, brick & 15
        side = (parity + zl + yl + (zl >> 3)) & 1
        h1 = side * 4 + (k >> 7)
        h2 = (1 - side) * 4 + (k >> 7)
        inside = (k2 >= 0) & (k2 < NX // 2)
        h3 = jnp.where(inside, (1 - side) * 4 + (k2 >> 7), -1)
        none = jnp.full(TILE, -1, I32)
        zero = jnp.zeros(TILE, F32)

        def swap(x):
            return pltpu.roll(x, 64, 1)

        def both(x, y):
            return (jnp.where(left, x, swap(y)), jnp.where(left, swap(x), y))

        lanes_ = both(k & 127, k2 & 127)
        ha, hb = both(h1, h3), both(h2, none)
        wa, wb = both(wm, beyond), both(beside, zero)
        vals = [both(v, v) for v in (n0, n1, n2, w)]
        for r in range(8):
            weights, onehots = [], []
            for s in range(S_PEER):
                def row(x):
                    return x[s][r : r + 1, :]

                unit = jnp.where(rank == row(ha), row(wa), jnp.where(rank == row(hb), row(wb), 0.0))
                weights.append(jnp.concatenate(parts(jnp.concatenate([unit * row(v) for v in vals], axis=0)), axis=0))
                onehots.append((wide_rank == row(lanes_)).astype(F32).astype(BF16))
            apart = jnp.zeros(weights[0].shape, BF16)
            diagonal = jnp.concatenate(
                [jnp.concatenate([weights[0], apart], axis=1), jnp.concatenate([apart, weights[1]], axis=1)], axis=0
            )
            out = lax.dot_general(
                diagonal, jnp.concatenate(onehots, axis=1), (((1,), (1,)), ((), ())), preferred_element_type=F32
            )
            for s in range(S_PEER):
                b = brick_s[g * 8 + r, s * CAP]
                acc[b] = acc[b] + (out[s * 64 : s * 64 + 32] + out[s * 64 + 32 : s * 64 + 64])
        return 0

    lax.fori_loop(0, sources // 8, group, 0)

    low = low_half((Y_DEV, *TILE))

    def fields(zp, ch):
        one = acc[pl.ds(zp * Y_DEV, Y_DEV), ch * 8 : ch * 8 + 8, :]
        two = acc[pl.ds((zp + HALF) * Y_DEV, Y_DEV), ch * 8 : ch * 8 + 8, :]
        return jnp.where(low, one, two), swap_halves(jnp.where(low, two, one))

    nil = jnp.zeros((1, *TILE), F32)
    for colour in range(2):
        for zp in range(HALF):
            f1[colour, zp, 0:1] = nil
            f1[colour, zp, Y_DEV + 1 : Y_DEV + 2] = nil

    def planes(pair, _):
        for odd in range(2):
            zp = pair * 2 + odd
            x = fields(zp, 0)
            y = fields(zp, 1)
            z = fields(zp, 2)
            d = fields(zp, 3)
            for colour in range(2):
                def slope(tiles, parity):
                    other = neighbour(tiles, parity)
                    return tiles - other if parity == 0 else other - tiles

                rhs_ref[colour, zp] = by_rows(x[1 - colour], (odd + colour) % 2, slope)
                f1[colour, zp, 1 : Y_DEV + 1] = y[colour]
                f2[colour, zp + 1] = z[colour]
                inv_ref[colour, zp] = 1.0 / (32.0 + 48.0 * d[colour])
                ysend_ref[0, 16 + colour * HALF + zp] = y[colour][0]
                ysend_ref[1, 16 + colour * HALF + zp] = y[colour][Y_DEV - 1]
        return 0

    lax.fori_loop(0, HALF // 2, planes, 0)
    zsend_ref[0, 16:32] = acc[0:Y_DEV, 16:24, :]
    zsend_ref[1, 16:32] = acc[(Z_DEV - 1) * Y_DEV :, 16:24, :]
    for colour in range(2):
        f2[colour, 0] = swap_halves(jnp.where(low, f2[colour, HALF], 0.0))
        f2[colour, HALF + 1] = swap_halves(jnp.where(low, 0.0, f2[colour, 1]))

    def finish(zp, _):
        for colour in range(2):
            o = 1 - colour
            spread = rhs_ref[colour, zp] + f1[o, zp, 2:] - f1[o, zp, :-2] + f2[o, zp + 2] - f2[o, zp]
            rhs_ref[colour, zp] = -6.0 * spread
        return 0

    lax.fori_loop(0, HALF, finish, 0)
    ends = (0, Y_DEV - 1)
    for s, y in enumerate(ends):
        ysend_ref[s, 0:HALF] = rhs_ref[0, :, y]
        ysend_ref[s, HALF : 2 * HALF] = inv_ref[0, :, y]
        for t in range(2):
            ysend_ref[s, 32 + t] = zsend_ref[t, 16 + y]
    for t, zp in enumerate((0, HALF - 1)):
        pack = pack_top if t == 1 else pack_bottom
        for q, ref in enumerate((rhs_ref, inv_ref)):
            zsend_ref[t, q * HALF : (q + 1) * HALF] = pack(ref[0, zp, :HALF], ref[0, zp, HALF:])
        for s, y in enumerate(ends):
            slope = f1[1, zp, y + 1]
            zsend_ref[t, 32 + s] = slope
            for q, tile in enumerate((rhs_ref[0, zp, y], inv_ref[0, zp, y], slope, zsend_ref[t, 16 + y])):
                csend_ref[2 * t + s, q] = tile


def relax_kernel(
    rhs_in, inv_in, start_ref, ysend_ref, zsend_ref, csend_ref, out_ref,
    v, edge, face, beside, red, red_inv, black, yin, zin, cin, send, recv, fsend, frecv,
):
    grid = Grid()
    grid.greet_neighbours()
    w, end = WIDE, WIDE + Y_DEV
    versions = [start_ref.at[0], start_ref.at[1]] + [v.at[n] for n in range(2 * SWEEPS - 1)]
    plans = [
        grid.halo(versions[n + 2], edge.at[n], face.at[n], beside.at[n // 2] if n % 2 == 0 else None)
        for n in range(2 * SWEEPS - 2)
    ]
    for plan in plans:
        grid.clear(landing(plan))
    fields = []
    for d in SIDES:
        to = [(int(x == 1), int(x != 1)) for x in d]
        if d[0] == 0:
            fields.append((d, ysend_ref.at[to[1][0]], yin.at[to[1][1]]))
        elif d[1] == 0:
            fields.append((d, zsend_ref.at[to[0][0]], zin.at[to[0][1]]))
        else:
            fields.append((d, csend_ref.at[2 * to[0][0] + to[1][0]], cin.at[2 * to[0][1] + to[1][1]]))
    grid.clear(landing(fields))
    for zp in range(HALF):
        red[zp + 1, 1 : Y_DEV + 1] = rhs_in[0, zp]
        red_inv[zp + 1, 1 : Y_DEV + 1] = inv_in[0, zp]
        black[zp] = rhs_in[1, zp]

    def update(step, plane, y, count):
        plane, parity = (plane, plane) if isinstance(plane, int) else plane
        same, opp, colour = versions[step], versions[step + 1], step % 2
        if colour == 0:
            right, scale = red[plane - 1, y - 1 : y - 1 + count], red_inv[plane - 1, y - 1 : y - 1 + count]
        else:
            right, scale = black[plane - w, y - w : y - w + count], inv_in[1, plane - w, y - w : y - w + count]
        s1 = same[plane - 1, y - 1 : y + count + 1] + same[plane + 1, y - 1 : y + count + 1]
        o1 = opp[plane - 1, y - 1 : y + count + 1] + opp[plane + 1, y - 1 : y + count + 1]
        s0 = same[plane, y - 1 : y + count + 1]
        around = s1[1:-1] + s0[:-2] + s0[2:]
        diagonal = s1[:-2] + s1[2:]
        across = 2.0 * around + (o1[:-2] + o1[2:])
        total = right + 2.0 * diagonal + across
        value = (total + by_rows(across, (parity + y + colour) % 2, neighbour)) * scale
        if step == 2 * SWEEPS - 1:
            out_ref[1, plane - w, y - w : y - w + count] = value
        else:
            versions[step + 2][plane, y : y + count] = value

    def inside(step, first, planes, y, count):
        def pair(i, _):
            for odd in range(2):
                update(step, (i * 2 + first + odd, first + odd), y, count)
            return 0

        lax.fori_loop(0, planes // 2, pair, 0)

    def red_inside(sweep):
        inside(2 * sweep, w + 1, HALF - 2, w + 1, Y_DEV - 2)

    def red_outside(sweep):
        for plane in (w - 1, w, w + HALF - 1, w + HALF):
            update(2 * sweep, plane, w - 1, Y_DEV + 2)
        for plane in range(w + 1, w + HALF - 1):
            for y in (w - 1, end - 1):
                update(2 * sweep, plane, y, 2)

    def black_outside(sweep):
        for plane in (w, w + 1, w + HALF - 2, w + HALF - 1):
            update(2 * sweep + 1, plane, w, Y_DEV)
        for plane in range(w + 2, w + HALF - 2):
            for y in (w, end - 2):
                update(2 * sweep + 1, plane, y, 2)

    def black_inside(sweep):
        inside(2 * sweep + 1, w + 2, HALF - 4, w + 2, Y_DEV - 4)

    red_inside(0)
    grid.await_neighbours()
    pairs = grid.copies(fields, fsend, frecv)
    grid.start(pairs)
    sent = [pairs]
    grid.take(pairs)

    for tiles, q in ((red, 0), (red_inv, 1)):
        for s, y in enumerate((0, Y_DEV + 1)):
            tiles[1 : HALF + 1, y] = yin[s, q * HALF : (q + 1) * HALF]
        sides = [
            jnp.concatenate([zin[t, q * HALF : (q + 1) * HALF], cin[2 * t, q : q + 1], cin[2 * t + 1, q : q + 1]], axis=0)
            for t in range(2)
        ]
        rim_planes(tiles, 1, 0, sides[0], sides[1])

    def slopes(own, below, above):
        return jnp.concatenate([under(own[HALF - 1 :], below), own, over(own[:1], above)], axis=0)

    inner_y = [slopes(ysend_ref[s, 24:32], zin[0, 32 + s : 33 + s], zin[1, 32 + s : 33 + s]) for s in range(2)]
    outer_y = [slopes(yin[s, 24:32], cin[s, 2:3], cin[2 + s, 2:3]) for s in range(2)]
    red[:, 0] -= 6.0 * inner_y[0]
    red[:, 1] += 6.0 * outer_y[0]
    red[:, Y_DEV] -= 6.0 * outer_y[1]
    red[:, Y_DEV + 1] += 6.0 * inner_y[1]
    black[:, 0] += 6.0 * yin[0, 16:24]
    black[:, Y_DEV - 1] -= 6.0 * yin[1, 16:24]

    low = low_half((Y_DEV + 2, *TILE))
    inner_z = [
        jnp.concatenate([yin[0, 32 + t : 33 + t], zsend_ref[t, 16:32], yin[1, 32 + t : 33 + t]], axis=0) for t in range(2)
    ]
    outer_z = [
        jnp.concatenate([cin[2 * t, 3:4], zin[t, 16:32], cin[2 * t + 1, 3:4]], axis=0) for t in range(2)
    ]
    red[0] -= jnp.where(low, 6.0 * swap_halves(inner_z[0]), 0.0)
    red[1] += jnp.where(low, 6.0 * outer_z[0], 0.0)
    red[HALF] -= jnp.where(low, 0.0, 6.0 * outer_z[1])
    red[HALF + 1] += jnp.where(low, 0.0, 6.0 * swap_halves(inner_z[1]))
    black[0] += jnp.where(low[1:-1], 6.0 * swap_halves(zin[0, 16:32]), 0.0)
    black[HALF - 1] -= jnp.where(low[1:-1], 0.0, 6.0 * swap_halves(zin[1, 16:32]))

    for sweep in range(SWEEPS):
        final = sweep == SWEEPS - 1
        news = (2 * sweep, 2 * sweep + 1)
        flying = []

        def launch(n):
            pack_faces(versions[n + 2], face.at[n])
            pairs = grid.copies(plans[n], send.at[n], recv.at[n])
            grid.start(pairs)
            flying.append(pairs)

        red_outside(sweep)
        if not final:
            launch(news[0])
        black_outside(sweep)
        if not final:
            launch(news[1])
        black_inside(sweep)
        if not final:
            red_inside(sweep + 1)
            for n, pairs in zip(news, flying):
                grid.take(pairs)
                if n % 2 == 0:
                    for s, y in enumerate((0, end)):
                        versions[n + 2][w : w + HALF, y : y + w] = beside[n // 2, s]
                rims(versions[n + 2], edge.at[n])
            sent += flying

    for zp in range(HALF):
        out_ref[0, zp] = versions[2 * SWEEPS][zp + w, w:end]
    for pairs in sent:
        grid.sent(pairs)


def interleave_kernel(in_ref, out_ref):
    col, row = iota((256, 256), 1), iota((256, 256), 0)
    place = (col == jnp.where(row < 128, 2 * row, 2 * row - 255)).astype(BF16)
    rows = Z_DEV * Y_DEV
    cells = iota((rows, 128), 0)
    even = (cells + cells // Y_DEV) % 2 == 0
    for i in range(4):
        colours = []
        for colour in range(2):
            base = [((colour * HALF + z % HALF) * Y_DEV) * 8 + (z // HALF) * 4 + i for z in range(Z_DEV)]
            colours.append(jnp.concatenate([in_ref[pl.ds(b, Y_DEV, stride=8), :] for b in base], axis=0))
        red, black = colours
        both = jnp.concatenate([jnp.where(even, red, black), jnp.where(even, black, red)], axis=1)
        high, low = parts(both)
        merged = jnp.dot(high, place, preferred_element_type=F32) + jnp.dot(low, place, preferred_element_type=F32)
        out_ref[:, :, 256 * i : 256 * (i + 1)] = merged.reshape(Z_DEV, Y_DEV, 256)


VM = pl.BlockSpec(memory_space=pltpu.VMEM)


def call(kernel, outs, scratch, specs, limit, **params):
    return pl.pallas_call(
        kernel,
        out_shape=outs,
        in_specs=specs,
        out_specs=jax.tree.map(lambda _: VM, outs),
        scratch_shapes=scratch,
        compiler_params=pltpu.CompilerParams(vmem_limit_bytes=limit << 20, **params),
    )


def shards(slot_brick, slot_count, point_cell, point_frac, point_normal, point_weight, guess):
    peers = point_cell.shape[1]
    full = jax.ShapeDtypeStruct((2, *FULL), F32)
    steps = 2 * SWEEPS - 1

    def last(x):
        return jnp.moveaxis(x[0], 0, -1)

    args = (last(slot_brick), last(slot_count), last(point_cell), last(point_frac), last(point_normal), last(point_weight), guess)
    points, start = call(
        bin_kernel,
        (jax.ShapeDtypeStruct((peers * 8, 128), F32), jax.ShapeDtypeStruct((2, *rimmed(WIDE)), F32)),
        [pltpu.VMEM(a.shape, a.dtype) for a in args]
        + [
            pltpu.VMEM((peers * 8, 128), F32),
            pltpu.VMEM((2 * HALF * Y_DEV * 8, 128), F32),
            pltpu.VMEM((2, *edge_shape(WIDE)), F32),
            pltpu.VMEM((2, 2, WIDE, HALF, *TILE), F32),
            pltpu.SemaphoreType.DMA((7,)),
            pltpu.SemaphoreType.DMA,
            pltpu.SemaphoreType.DMA,
            pltpu.SemaphoreType.DMA((2, 8)),
            pltpu.SemaphoreType.DMA((2, 8)),
        ],
        [pl.BlockSpec(memory_space=pltpu.HBM)] * 7,
        24,
        collective_id=0,
        has_side_effects=True,
    )(*[pltpu.with_memory_space_constraint(a, pltpu.HBM) for a in args])
    outs = (
        full,
        full,
        jax.ShapeDtypeStruct((2, 34, *TILE), F32),
        jax.ShapeDtypeStruct((2, 34, *TILE), F32),
        jax.ShapeDtypeStruct((4, 4, *TILE), F32),
    )
    rhs, inv, ysend, zsend, csend = call(
        splat_kernel,
        outs,
        [
            pltpu.VMEM((Z_DEV * Y_DEV, 32, 128), F32),
            pltpu.VMEM((peers, 128), I32),
            pltpu.SMEM((peers, 128), I32),
            pltpu.VMEM((2, HALF, Y_DEV + 2, *TILE), F32),
            pltpu.VMEM((2, HALF + 2, Y_DEV, *TILE), F32),
            pltpu.SemaphoreType.DMA,
        ],
        [VM],
        32,
    )(points)
    relaxed = call(
        relax_kernel,
        full,
        [
            pltpu.VMEM((steps, *rimmed(WIDE)), F32),
            pltpu.VMEM((steps - 1, *edge_shape(WIDE)), F32),
            pltpu.VMEM((steps - 1, 2, WIDE, HALF, *TILE), F32),
            pltpu.VMEM((SWEEPS - 1, 2, HALF, WIDE, *TILE), F32),
            pltpu.VMEM(rimmed(1), F32),
            pltpu.VMEM(rimmed(1), F32),
            pltpu.VMEM(FULL, F32),
            pltpu.VMEM((2, 34, *TILE), F32),
            pltpu.VMEM((2, 34, *TILE), F32),
            pltpu.VMEM((4, 4, *TILE), F32),
            pltpu.SemaphoreType.DMA((steps - 1, 8)),
            pltpu.SemaphoreType.DMA((steps - 1, 8)),
            pltpu.SemaphoreType.DMA((8,)),
            pltpu.SemaphoreType.DMA((8,)),
        ],
        [VM] * 6,
        32,
        collective_id=1,
        has_side_effects=True,
    )(rhs, inv, start, ysend, zsend, csend)
    return call(interleave_kernel, jax.ShapeDtypeStruct((Z_DEV, Y_DEV, NX), F32), [], [VM], 16)(relaxed.reshape(-1, 128))


def solution(mesh):
    placed = (
        P(("slab", "row"), None, None),
        P(("slab", "row"), None, None),
        P(("slab", "row"), None, None, None),
        P(("slab", "row"), None, None, None),
        P(("slab", "row"), None, None, None, None),
        P(("slab", "row"), None, None, None),
        P("slab", "row", None),
    )
    return jax.shard_map(
        shards, mesh=mesh, in_specs=placed, out_specs=P("slab", "row", None), check_vma=False
    )
```

```python
import functools

import jax
import jax.numpy as jnp
from jax import lax
from jax.experimental import pallas as pl
from jax.experimental.pallas import tpu as pltpu
from jax.sharding import PartitionSpec as P

Z_DEV = 16
Y_DEV = 16
NX = 1024
CAP = 64
S_PEER = 2
SWEEPS = 3
HALF = Z_DEV // 2
TILE = (8, 128)
MESH = pl.DeviceIdType.MESH
LOGICAL = pl.DeviceIdType.LOGICAL
F32 = jnp.float32
BF16 = jnp.bfloat16
I32 = jnp.int32


def iota(shape, dim):
    return lax.broadcasted_iota(I32, shape, dim)


def swap_halves(tiles):
    return pltpu.roll(tiles, 4, tiles.ndim - 2)


def low_half(shape):
    return iota(shape, len(shape) - 2) < 4


def neighbour(tiles, parity):
    shape = tiles.shape
    lane, sub = iota(shape, len(shape) - 1), iota(shape, len(shape) - 2) % 4
    if parity == 0:
        near = pltpu.roll(tiles, 1, len(shape) - 1)
        far = pltpu.roll(near, 1, len(shape) - 2)
        edge, end = lane == 0, sub == 0
    else:
        near = pltpu.roll(tiles, 127, len(shape) - 1)
        far = pltpu.roll(near, 7, len(shape) - 2)
        edge, end = lane == 127, sub == 3
    return jnp.where(edge, jnp.where(end, 0.0, far), near)


def by_rows(tiles, parity, function):
    pairs = tiles.reshape(tiles.shape[0] // 2, 2, *TILE)
    done = [function(pairs[:, q], (parity + q) % 2) for q in range(2)]
    return jnp.stack(done, axis=1).reshape(tiles.shape)


def parts(x):
    high = x.astype(BF16)
    return high, (x - high.astype(F32)).astype(BF16)


def deinterleave(guess_ref, start_ref):
    col, row = iota((256, 256), 1), iota((256, 256), 0)
    place = (row == jnp.where(col < 128, 2 * col, 2 * col - 255)).astype(BF16)
    rows = Z_DEV * Y_DEV
    cells = iota((rows, 128), 0)
    even = (cells + cells // Y_DEV) % 2 == 0
    for i in range(4):
        chunk = guess_ref[:, :, 256 * i : 256 * (i + 1)].reshape(rows, 256)
        high, low = parts(chunk)
        split = jnp.dot(high, place, preferred_element_type=F32) + jnp.dot(low, place, preferred_element_type=F32)
        first, second = split[:, :128], split[:, 128:]
        colours = (jnp.where(even, first, second), jnp.where(even, second, first))
        for colour in range(2):
            for z in range(Z_DEV):
                base = ((colour * HALF + z % HALF) * Y_DEV) * 8 + (z // HALF) * 4 + i
                start_ref[pl.ds(base, Y_DEV, stride=8), :] = colours[colour][z * Y_DEV : (z + 1) * Y_DEV]


SIDES = [(1, 1), (1, -1), (-1, 1), (-1, -1), (1, 0), (-1, 0), (0, 1), (0, -1)]
WIDE = 2
ROWS = 7
FULL = (HALF, Y_DEV, *TILE)


def rimmed(width):
    return (HALF + 2 * width, Y_DEV + 2 * width, *TILE)


def edge_shape(width):
    return (2, width, HALF + 2 * width, *TILE)


class Grid:
    def __init__(self):
        self.ns, self.nr = lax.axis_size("slab"), lax.axis_size("row")
        self.slab, self.line = lax.axis_index("slab"), lax.axis_index("row")

    def exists(self, d):
        tests = []
        for step, at, size in ((d[0], self.slab, self.ns), (d[1], self.line, self.nr)):
            if step == 1:
                tests.append(at < size - 1)
            if step == -1:
                tests.append(at > 0)
        return tests[0] if len(tests) == 1 else tests[0] & tests[1]

    def device(self, d):
        return (self.slab + d[0], self.line + d[1])

    def greet_neighbours(self):
        barrier = pltpu.get_barrier_semaphore()
        for d in SIDES:
            @pl.when(self.exists(d))
            def _():
                pl.semaphore_signal(barrier, inc=1, device_id=self.device(d), device_id_type=MESH)

    def await_neighbours(self):
        counts = [
            1 + (at > 0).astype(I32) + (at < size - 1).astype(I32)
            for at, size in ((self.slab, self.ns), (self.line, self.nr))
        ]
        pl.semaphore_wait(pltpu.get_barrier_semaphore(), counts[0] * counts[1] - 1)

    def start(self, pairs):
        for d, copy in pairs:
            @pl.when(self.exists(d))
            def _():
                copy.start()

    def take(self, pairs):
        for d, copy in pairs:
            @pl.when(self.exists((-d[0], -d[1])))
            def _():
                copy.wait_recv()

    def sent(self, pairs):
        for d, copy in pairs:
            @pl.when(self.exists(d))
            def _():
                copy.wait_send()

    def clear(self, pairs):
        for d, dst in pairs:
            @pl.when(jnp.logical_not(self.exists((-d[0], -d[1]))))
            def _():
                dst[...] = jnp.zeros(dst.shape, F32)

    def halo(self, tiles, edge, face, beside=None):
        w = WIDE
        ends = {1: pl.ds(Y_DEV, w), -1: pl.ds(w, w)}
        plan = []
        for d in SIDES:
            side = 0 if d[0] == 1 else 1
            if d[0] == 0:
                dst = tiles.at[pl.ds(w, HALF), pl.ds(0 if d[1] == 1 else Y_DEV + w, w)]
                if beside is not None:
                    dst = beside.at[0 if d[1] == 1 else 1]
                plan.append((d, tiles.at[pl.ds(w, HALF), ends[d[1]]], dst))
            elif d[1] == 0:
                plan.append((d, face.at[side], edge.at[side, pl.ds(0, w), pl.ds(0, HALF)]))
            else:
                dst = edge.at[side, pl.ds(0, w), pl.ds(HALF if d[1] == 1 else HALF + w, w)]
                plan.append((d, tiles.at[pl.ds(HALF if d[0] == 1 else w, w), ends[d[1]]], dst))
        return plan

    def copies(self, plan, send, recv):
        return [
            (d, pltpu.make_async_remote_copy(src, dst, send.at[q], recv.at[q], self.device(d), MESH))
            for q, (d, src, dst) in enumerate(plan)
        ]


def landing(plan):
    return [(d, dst) for d, _, dst in plan]


def pack_top(first, second):
    return jnp.where(low_half(first.shape), swap_halves(first), second)


def pack_bottom(first, second):
    return jnp.where(low_half(first.shape), first, swap_halves(second))


def pack_faces(tiles, face):
    w, half = WIDE, WIDE + HALF
    for p in range(w):
        face[0, p] = pack_top(tiles[HALF + p, w:half], tiles[HALF + p, half : half + HALF])
        face[1, p] = pack_bottom(tiles[w + p, w:half], tiles[w + p, half : half + HALF])


def under(own, corner):
    return swap_halves(jnp.where(low_half(own.shape), own, corner))


def over(own, corner):
    return swap_halves(jnp.where(low_half(own.shape), corner, own))


def rim_planes(tiles, w, p, below, above):
    half = w + HALF
    first, second = slice(w, half), slice(half, half + HALF)
    top, bottom = tiles[HALF + p], tiles[w + p]
    low = low_half((HALF, *TILE))
    up, down = p, HALF + w + p
    tiles[up, first] = jnp.where(low, below[:HALF], swap_halves(top[first]))
    tiles[up, second] = swap_halves(jnp.where(low, top[second], below[:HALF]))
    tiles[down, first] = swap_halves(jnp.where(low, above[:HALF], bottom[first]))
    tiles[down, second] = jnp.where(low, swap_halves(bottom[second]), above[:HALF])
    for y, at in ((slice(0, w), slice(HALF, half)), (slice(Y_DEV + w, Y_DEV + 2 * w), slice(half, half + w))):
        tiles[up, y] = under(top[y], below[at])
        tiles[down, y] = over(bottom[y], above[at])


def rims(tiles, edge):
    for p in range(WIDE):
        rim_planes(tiles, WIDE, p, edge[0, p], edge[1, p])


def bin_kernel(
    brick_in, count_in, cell_in, frac_in, normal_in, weight_in, guess_in, points_ref, v_ref,
    brick_ref, count_ref, cell_ref, frac_ref, normal_ref, weight_ref, guess_ref,
    packed, split, edge, face, load, psend, precv, send, recv,
):
    loads = [
        pltpu.make_async_copy(src, dst, load.at[q])
        for q, (src, dst) in enumerate(
            (
                (guess_in, guess_ref), (brick_in, brick_ref), (count_in, count_ref), (cell_in, cell_ref),
                (frac_in, frac_ref), (normal_in, normal_ref), (weight_in, weight_ref),
            )
        )
    ]
    for copy in loads:
        copy.start()
    grid = Grid()
    peers = grid.ns * grid.nr
    me = grid.slab * grid.nr + grid.line
    barrier = pltpu.get_barrier_semaphore()
    plans = [grid.halo(v_ref.at[c], edge.at[c], face.at[c]) for c in range(2)]
    for plan in plans:
        grid.clear(landing(plan))

    sizes = (4, 4, 2, 4) if peers == 128 else (1, 1, grid.ns, grid.nr)
    strides = [sizes[1] * sizes[2] * sizes[3], sizes[2] * sizes[3], sizes[3], 1]
    shifted = [
        [lax.rem(lax.rem(me // stride, size) + k, size) * stride for k in range(size)]
        for stride, size in zip(strides, sizes)
    ]
    steps = [(z, x, c, y) for z in range(sizes[0]) for x in range(sizes[1]) for c in range(sizes[2]) for y in range(sizes[3])]
    hops = {o: sum(min(k, size - k) for k, size in zip(o, sizes)) for o in steps}
    order = sorted(steps[1:], key=lambda o: -hops[o])

    def peer(o):
        return sum(column[k] for column, k in zip(shifted, o))

    for o in order:
        pl.semaphore_signal(barrier, inc=1, device_id=peer(o), device_id_type=LOGICAL)

    loads[0].wait()
    deinterleave(guess_ref, split)
    for colour in range(2):
        for zp in range(HALF):
            at = (colour * HALF + zp) * Y_DEV * 8
            v_ref[colour, zp + WIDE, WIDE : WIDE + Y_DEV] = split[at : at + Y_DEV * 8, :].reshape(Y_DEV, *TILE)
        pack_faces(v_ref.at[colour], face.at[colour])
    for copy in loads[1:]:
        copy.wait()

    point = iota((CAP, peers), 0)
    live = jnp.concatenate([(point < count_ref[s : s + 1, :]).astype(F32) for s in range(S_PEER)], axis=0)

    def put(r, first, second, mask=None):
        both = jnp.concatenate([first, second], axis=0).astype(F32)
        packed[pl.ds(r, peers, stride=8), :] = (both if mask is None else both * mask).T

    put(0, cell_ref[0], cell_ref[1])
    put(1, frac_ref[0], frac_ref[1])
    for ch in range(3):
        put(2 + ch, normal_ref[0, ch], normal_ref[1, ch], live)
    put(5, weight_ref[0], weight_ref[1], live)
    put(6, *[jnp.broadcast_to(brick_ref[s : s + 1, :], point.shape) for s in range(S_PEER)])

    def rows(t):
        return pl.ds(pl.multiple_of(t * 8, 8), ROWS)

    pl.semaphore_wait(barrier, peers - 1)

    for o in order:
        t = peer(o)
        pltpu.make_async_remote_copy(packed.at[rows(t)], points_ref.at[rows(me)], psend, precv, t, LOGICAL).start()
    halos = [grid.copies(plans[c], send.at[c], recv.at[c]) for c in range(2)]
    for colour in range(2):
        grid.start(halos[colour])
    points_ref[rows(me), :] = packed[rows(me), :]
    for colour in range(2):
        grid.take(halos[colour])
        rims(v_ref.at[colour], edge.at[colour])
    others = pl.ds(0, (peers - 1) * ROWS)
    every = pltpu.make_async_remote_copy(packed.at[others], points_ref.at[others], psend, precv, peer(order[-1]), LOGICAL)
    every.wait_recv()
    every.wait_send()
    for colour in range(2):
        grid.sent(halos[colour])


def splat_kernel(points_ref, rhs_ref, inv_ref, ysend_ref, zsend_ref, csend_ref, acc, brick_v, brick_s, f1, f2, sem):
    sources = points_ref.shape[0] // 8
    brick_v[...] = points_ref[pl.ds(6, sources, stride=8), :].astype(I32)
    copy = pltpu.make_async_copy(brick_v, brick_s, sem)
    copy.start()

    def clear(b, _):
        acc[pl.ds(b * 8, 8)] = jnp.zeros((8, 32, 128), F32)
        return 0

    lax.fori_loop(0, Z_DEV * Y_DEV // 8, clear, 0)
    copy.wait()

    lane = iota(TILE, 1)
    left = lane < CAP
    rank = iota(TILE, 0)
    wide_rank = iota((128, 128), 0)

    def group(g, _):
        cell, frac, n0, n1, n2, w, brick = [points_ref[pl.ds(g * 64 + r, 8, stride=8), :] for r in range(7)]
        cell, brick = cell.astype(I32), brick.astype(I32)
        parity, k = cell & 1, cell >> 1
        even = parity == 0
        wl = 0.5 * (0.5 - frac) * (0.5 - frac)
        wm = 0.75 - frac * frac
        wh = 0.5 * (0.5 + frac) * (0.5 + frac)
        beside = jnp.where(even, wh, wl)
        beyond = jnp.where(even, wl, wh)
        k2 = jnp.where(even, k - 1, k + 1)
        zl, yl = brick >> 4, brick & 15
        side = (parity + zl + yl + (zl >> 3)) & 1
        h1 = side * 4 + (k >> 7)
        h2 = (1 - side) * 4 + (k >> 7)
        inside = (k2 >= 0) & (k2 < NX // 2)
        h3 = jnp.where(inside, (1 - side) * 4 + (k2 >> 7), -1)
        none = jnp.full(TILE, -1, I32)
        zero = jnp.zeros(TILE, F32)

        def swap(x):
            return pltpu.roll(x, 64, 1)

        def both(x, y):
            return (jnp.where(left, x, swap(y)), jnp.where(left, swap(x), y))

        lanes_ = both(k & 127, k2 & 127)
        ha, hb = both(h1, h3), both(h2, none)
        wa, wb = both(wm, beyond), both(beside, zero)
        vals = [both(v, v) for v in (n0, n1, n2, w)]
        for r in range(8):
            weights, onehots = [], []
            for s in range(S_PEER):
                def row(x):
                    return x[s][r : r + 1, :]

                unit = jnp.where(rank == row(ha), row(wa), jnp.where(rank == row(hb), row(wb), 0.0))
                weights.append(jnp.concatenate(parts(jnp.concatenate([unit * row(v) for v in vals], axis=0)), axis=0))
                onehots.append((wide_rank == row(lanes_)).astype(F32).astype(BF16))
            apart = jnp.zeros(weights[0].shape, BF16)
            diagonal = jnp.concatenate(
                [jnp.concatenate([weights[0], apart], axis=1), jnp.concatenate([apart, weights[1]], axis=1)], axis=0
            )
            out = lax.dot_general(
                diagonal, jnp.concatenate(onehots, axis=1), (((1,), (1,)), ((), ())), preferred_element_type=F32
            )
            for s in range(S_PEER):
                b = brick_s[g * 8 + r, s * CAP]
                acc[b] = acc[b] + (out[s * 64 : s * 64 + 32] + out[s * 64 + 32 : s * 64 + 64])
        return 0

    lax.fori_loop(0, sources // 8, group, 0, unroll=min(8, sources // 8))

    low = low_half((Y_DEV, *TILE))

    def fields(zp, ch):
        one = acc[pl.ds(zp * Y_DEV, Y_DEV), ch * 8 : ch * 8 + 8, :]
        two = acc[pl.ds((zp + HALF) * Y_DEV, Y_DEV), ch * 8 : ch * 8 + 8, :]
        return jnp.where(low, one, two), swap_halves(jnp.where(low, two, one))

    nil = jnp.zeros((1, *TILE), F32)
    for colour in range(2):
        for zp in range(HALF):
            f1[colour, zp, 0:1] = nil
            f1[colour, zp, Y_DEV + 1 : Y_DEV + 2] = nil

    def planes(pair, _):
        for odd in range(2):
            zp = pair * 2 + odd
            x = fields(zp, 0)
            y = fields(zp, 1)
            z = fields(zp, 2)
            d = fields(zp, 3)
            for colour in range(2):
                def slope(tiles, parity):
                    other = neighbour(tiles, parity)
                    return tiles - other if parity == 0 else other - tiles

                rhs_ref[colour, zp] = by_rows(x[1 - colour], (odd + colour) % 2, slope)
                f1[colour, zp, 1 : Y_DEV + 1] = y[colour]
                f2[colour, zp + 1] = z[colour]
                inv_ref[colour, zp] = 1.0 / (32.0 + 48.0 * d[colour])
                ysend_ref[0, (26, 16)[colour] + zp] = y[colour][0]
                ysend_ref[1, (26, 16)[colour] + zp] = y[colour][Y_DEV - 1]
        return 0

    lax.fori_loop(0, HALF // 2, planes, 0)
    zsend_ref[0, 16:32] = acc[0:Y_DEV, 16:24, :]
    zsend_ref[1, 16:32] = acc[(Z_DEV - 1) * Y_DEV :, 16:24, :]
    for colour in range(2):
        f2[colour, 0] = swap_halves(jnp.where(low, f2[colour, HALF], 0.0))
        f2[colour, HALF + 1] = swap_halves(jnp.where(low, 0.0, f2[colour, 1]))

    def finish(zp, _):
        for colour in range(2):
            o = 1 - colour
            spread = rhs_ref[colour, zp] + f1[o, zp, 2:] - f1[o, zp, :-2] + f2[o, zp + 2] - f2[o, zp]
            rhs_ref[colour, zp] = -6.0 * spread
        return 0

    lax.fori_loop(0, HALF, finish, 0)
    ends = (0, Y_DEV - 1)
    for s, y in enumerate(ends):
        ysend_ref[s, 0:HALF] = rhs_ref[0, :, y]
        ysend_ref[s, HALF : 2 * HALF] = inv_ref[0, :, y]
        for t in range(2):
            ysend_ref[s, 24 + t] = zsend_ref[t, 16 + y]
    for t, zp in enumerate((0, HALF - 1)):
        pack = pack_top if t == 1 else pack_bottom
        for q, ref in enumerate((rhs_ref, inv_ref)):
            zsend_ref[t, q * HALF : (q + 1) * HALF] = pack(ref[0, zp, :HALF], ref[0, zp, HALF:])
        for s, y in enumerate(ends):
            slope = f1[1, zp, y + 1]
            zsend_ref[t, 32 + s] = slope
            for q, tile in enumerate((rhs_ref[0, zp, y], inv_ref[0, zp, y], slope, zsend_ref[t, 16 + y])):
                csend_ref[2 * t + s, q] = tile


def relax_kernel(
    rhs_in, inv_in, start_ref, ysend_ref, zsend_ref, csend_ref, out_ref,
    v, edge, face, beside, red, red_inv, black, yin, zin, cin, send, recv, fsend, frecv, lsend, lrecv,
):
    grid = Grid()
    grid.greet_neighbours()
    w, end = WIDE, WIDE + Y_DEV
    versions = [start_ref.at[0], start_ref.at[1]] + [v.at[n] for n in range(2 * SWEEPS - 1)]
    plans = [
        grid.halo(versions[n + 2], edge.at[n], face.at[n], beside.at[n // 2] if n % 2 == 0 else None)
        for n in range(2 * SWEEPS - 2)
    ]
    for plan in plans:
        grid.clear(landing(plan))
    fields, late = [], []
    for d in SIDES:
        to = [(int(x == 1), int(x != 1)) for x in d]
        if d[0] == 0:
            for plan, part in ((fields, pl.ds(0, 26)), (late, pl.ds(26, 8))):
                plan.append((d, ysend_ref.at[to[1][0], part], yin.at[to[1][1], part]))
        elif d[1] == 0:
            fields.append((d, zsend_ref.at[to[0][0]], zin.at[to[0][1]]))
        else:
            fields.append((d, csend_ref.at[2 * to[0][0] + to[1][0]], cin.at[2 * to[0][1] + to[1][1]]))
    grid.clear(landing(fields) + landing(late))
    for zp in range(HALF):
        red[zp + 1, 1 : Y_DEV + 1] = rhs_in[0, zp]
        red_inv[zp + 1, 1 : Y_DEV + 1] = inv_in[0, zp]
        black[zp] = rhs_in[1, zp]

    def update(step, plane, y, count):
        plane, parity = (plane, plane) if isinstance(plane, int) else plane
        same, opp, colour = versions[step], versions[step + 1], step % 2
        if colour == 0:
            right, scale = red[plane - 1, y - 1 : y - 1 + count], red_inv[plane - 1, y - 1 : y - 1 + count]
        else:
            right, scale = black[plane - w, y - w : y - w + count], inv_in[1, plane - w, y - w : y - w + count]
        s1 = same[plane - 1, y - 1 : y + count + 1] + same[plane + 1, y - 1 : y + count + 1]
        o1 = opp[plane - 1, y - 1 : y + count + 1] + opp[plane + 1, y - 1 : y + count + 1]
        s0 = same[plane, y - 1 : y + count + 1]
        around = s1[1:-1] + s0[:-2] + s0[2:]
        diagonal = s1[:-2] + s1[2:]
        across = 2.0 * around + (o1[:-2] + o1[2:])
        total = right + 2.0 * diagonal + across
        value = (total + by_rows(across, (parity + y + colour) % 2, neighbour)) * scale
        if step == 2 * SWEEPS - 1:
            out_ref[1, plane - w, y - w : y - w + count] = value
        else:
            versions[step + 2][plane, y : y + count] = value

    def inside(step, first, planes, y, count):
        def pair(i, _):
            for odd in range(2):
                update(step, (i * 2 + first + odd, first + odd), y, count)
            return 0

        lax.fori_loop(0, planes // 2, pair, 0)

    def red_inside(sweep):
        inside(2 * sweep, w + 1, HALF - 2, w + 1, Y_DEV - 2)

    def red_faces(sweep):
        for plane in (w, w + HALF - 1):
            update(2 * sweep, plane, w - 1, Y_DEV + 2)
        for plane in range(w + 1, w + HALF - 1):
            for y in (w - 1, end - 1):
                update(2 * sweep, plane, y, 2)

    def red_ring(sweep):
        for plane in (w - 1, w + HALF):
            update(2 * sweep, plane, w - 1, Y_DEV + 2)

    def black_faces(sweep):
        for plane in (w, w + HALF - 1):
            update(2 * sweep + 1, plane, w, Y_DEV)
        for plane in range(w + 1, w + HALF - 1):
            for y in (w, end - 2):
                update(2 * sweep + 1, plane, y, 2)

    def black_second(sweep):
        for plane in (w + 1, w + HALF - 2):
            update(2 * sweep + 1, plane, w + 2, Y_DEV - 4)

    def black_inside(sweep):
        inside(2 * sweep + 1, w + 2, HALF - 4, w + 2, Y_DEV - 4)

    red_inside(0)
    grid.await_neighbours()
    pairs = grid.copies(fields, fsend, frecv)
    tail = grid.copies(late, lsend, lrecv)
    grid.start(pairs + tail)
    sent = [pairs, tail]
    grid.take(pairs)

    for tiles, q in ((red, 0), (red_inv, 1)):
        for s, y in enumerate((0, Y_DEV + 1)):
            tiles[1 : HALF + 1, y] = yin[s, q * HALF : (q + 1) * HALF]
        sides = [
            jnp.concatenate([zin[t, q * HALF : (q + 1) * HALF], cin[2 * t, q : q + 1], cin[2 * t + 1, q : q + 1]], axis=0)
            for t in range(2)
        ]
        rim_planes(tiles, 1, 0, sides[0], sides[1])

    def slopes(own, below, above):
        return jnp.concatenate([under(own[HALF - 1 :], below), own, over(own[:1], above)], axis=0)

    inner_y = [slopes(ysend_ref[s, 16:24], zin[0, 32 + s : 33 + s], zin[1, 32 + s : 33 + s]) for s in range(2)]
    outer_y = [slopes(yin[s, 16:24], cin[s, 2:3], cin[2 + s, 2:3]) for s in range(2)]
    red[:, 0] -= 6.0 * inner_y[0]
    red[:, 1] += 6.0 * outer_y[0]
    red[:, Y_DEV] -= 6.0 * outer_y[1]
    red[:, Y_DEV + 1] += 6.0 * inner_y[1]

    low = low_half((Y_DEV + 2, *TILE))
    inner_z = [
        jnp.concatenate([yin[0, 24 + t : 25 + t], zsend_ref[t, 16:32], yin[1, 24 + t : 25 + t]], axis=0) for t in range(2)
    ]
    outer_z = [
        jnp.concatenate([cin[2 * t, 3:4], zin[t, 16:32], cin[2 * t + 1, 3:4]], axis=0) for t in range(2)
    ]
    red[0] -= jnp.where(low, 6.0 * swap_halves(inner_z[0]), 0.0)
    red[1] += jnp.where(low, 6.0 * outer_z[0], 0.0)
    red[HALF] -= jnp.where(low, 0.0, 6.0 * outer_z[1])
    red[HALF + 1] += jnp.where(low, 0.0, 6.0 * swap_halves(inner_z[1]))
    black[0] += jnp.where(low[1:-1], 6.0 * swap_halves(zin[0, 16:32]), 0.0)
    black[HALF - 1] -= jnp.where(low[1:-1], 0.0, 6.0 * swap_halves(zin[1, 16:32]))

    for sweep in range(SWEEPS):
        final = sweep == SWEEPS - 1
        news = (2 * sweep, 2 * sweep + 1)
        flying = []

        def launch(n, between):
            pairs = grid.copies(plans[n], send.at[n], recv.at[n])
            between(sweep)
            pack_faces(versions[n + 2], face.at[n])
            grid.start(pairs)
            flying.append(pairs)

        red_faces(sweep)
        if not final:
            launch(news[0], lambda _: None)
        red_ring(sweep)
        if sweep == 0:
            grid.take(tail)
            black[:, 0] += 6.0 * yin[0, 26:34]
            black[:, Y_DEV - 1] -= 6.0 * yin[1, 26:34]
        black_faces(sweep)
        if not final:
            launch(news[1], black_second)
        else:
            black_second(sweep)
        black_inside(sweep)
        if not final:
            red_inside(sweep + 1)
            for n, pairs in zip(news, flying):
                grid.take(pairs)
                if n % 2 == 0:
                    for s, y in enumerate((0, end)):
                        versions[n + 2][w : w + HALF, y : y + w] = beside[n // 2, s]
                rims(versions[n + 2], edge.at[n])
            sent += flying

    for zp in range(HALF):
        out_ref[0, zp] = versions[2 * SWEEPS][zp + w, w:end]
    for pairs in sent:
        grid.sent(pairs)


def interleave_kernel(in_ref, out_ref):
    col, row = iota((256, 256), 1), iota((256, 256), 0)
    place = (col == jnp.where(row < 128, 2 * row, 2 * row - 255)).astype(BF16)
    rows = Z_DEV * Y_DEV
    cells = iota((rows, 128), 0)
    even = (cells + cells // Y_DEV) % 2 == 0
    for i in range(4):
        colours = []
        for colour in range(2):
            base = [((colour * HALF + z % HALF) * Y_DEV) * 8 + (z // HALF) * 4 + i for z in range(Z_DEV)]
            colours.append(jnp.concatenate([in_ref[pl.ds(b, Y_DEV, stride=8), :] for b in base], axis=0))
        red, black = colours
        both = jnp.concatenate([jnp.where(even, red, black), jnp.where(even, black, red)], axis=1)
        high, low = parts(both)
        merged = jnp.dot(high, place, preferred_element_type=F32) + jnp.dot(low, place, preferred_element_type=F32)
        out_ref[:, :, 256 * i : 256 * (i + 1)] = merged.reshape(Z_DEV, Y_DEV, 256)


VM = pl.BlockSpec(memory_space=pltpu.VMEM)


def call(kernel, outs, scratch, specs, limit, **params):
    return pl.pallas_call(
        kernel,
        out_shape=outs,
        in_specs=specs,
        out_specs=jax.tree.map(lambda _: VM, outs),
        scratch_shapes=scratch,
        compiler_params=pltpu.CompilerParams(vmem_limit_bytes=limit << 20, **params),
    )


def shards(slot_brick, slot_count, point_cell, point_frac, point_normal, point_weight, guess):
    peers = point_cell.shape[1]
    full = jax.ShapeDtypeStruct((2, *FULL), F32)
    steps = 2 * SWEEPS - 1

    def last(x):
        return jnp.moveaxis(x[0], 0, -1)

    args = (last(slot_brick), last(slot_count), last(point_cell), last(point_frac), last(point_normal), last(point_weight), guess)
    points, start = call(
        bin_kernel,
        (jax.ShapeDtypeStruct((peers * 8, 128), F32), jax.ShapeDtypeStruct((2, *rimmed(WIDE)), F32)),
        [pltpu.VMEM(a.shape, a.dtype) for a in args]
        + [
            pltpu.VMEM((peers * 8, 128), F32),
            pltpu.VMEM((2 * HALF * Y_DEV * 8, 128), F32),
            pltpu.VMEM((2, *edge_shape(WIDE)), F32),
            pltpu.VMEM((2, 2, WIDE, HALF, *TILE), F32),
            pltpu.SemaphoreType.DMA((7,)),
            pltpu.SemaphoreType.DMA,
            pltpu.SemaphoreType.DMA,
            pltpu.SemaphoreType.DMA((2, 8)),
            pltpu.SemaphoreType.DMA((2, 8)),
        ],
        [pl.BlockSpec(memory_space=pltpu.HBM)] * 7,
        24,
        collective_id=0,
        has_side_effects=True,
    )(*[pltpu.with_memory_space_constraint(a, pltpu.HBM) for a in args])
    outs = (
        full,
        full,
        jax.ShapeDtypeStruct((2, 34, *TILE), F32),
        jax.ShapeDtypeStruct((2, 34, *TILE), F32),
        jax.ShapeDtypeStruct((4, 4, *TILE), F32),
    )
    rhs, inv, ysend, zsend, csend = call(
        splat_kernel,
        outs,
        [
            pltpu.VMEM((Z_DEV * Y_DEV, 32, 128), F32),
            pltpu.VMEM((peers, 128), I32),
            pltpu.SMEM((peers, 128), I32),
            pltpu.VMEM((2, HALF, Y_DEV + 2, *TILE), F32),
            pltpu.VMEM((2, HALF + 2, Y_DEV, *TILE), F32),
            pltpu.SemaphoreType.DMA,
        ],
        [VM],
        32,
    )(points)
    relaxed = call(
        relax_kernel,
        full,
        [
            pltpu.VMEM((steps, *rimmed(WIDE)), F32),
            pltpu.VMEM((steps - 1, *edge_shape(WIDE)), F32),
            pltpu.VMEM((steps - 1, 2, WIDE, HALF, *TILE), F32),
            pltpu.VMEM((SWEEPS - 1, 2, HALF, WIDE, *TILE), F32),
            pltpu.VMEM(rimmed(1), F32),
            pltpu.VMEM(rimmed(1), F32),
            pltpu.VMEM(FULL, F32),
            pltpu.VMEM((2, 34, *TILE), F32),
            pltpu.VMEM((2, 34, *TILE), F32),
            pltpu.VMEM((4, 4, *TILE), F32),
            pltpu.SemaphoreType.DMA((steps - 1, 8)),
            pltpu.SemaphoreType.DMA((steps - 1, 8)),
            pltpu.SemaphoreType.DMA((8,)),
            pltpu.SemaphoreType.DMA((8,)),
            pltpu.SemaphoreType.DMA((2,)),
            pltpu.SemaphoreType.DMA((2,)),
        ],
        [VM] * 6,
        32,
        collective_id=1,
        has_side_effects=True,
    )(rhs, inv, start, ysend, zsend, csend)
    return call(interleave_kernel, jax.ShapeDtypeStruct((Z_DEV, Y_DEV, NX), F32), [], [VM], 16)(relaxed.reshape(-1, 128))


def solution(mesh):
    placed = (
        P(("slab", "row"), None, None),
        P(("slab", "row"), None, None),
        P(("slab", "row"), None, None, None),
        P(("slab", "row"), None, None, None),
        P(("slab", "row"), None, None, None, None),
        P(("slab", "row"), None, None, None),
        P("slab", "row", None),
    )
    return jax.shard_map(
        shards, mesh=mesh, in_specs=placed, out_specs=P("slab", "row", None), check_vma=False
    )
```

```python
import functools

import jax
import jax.numpy as jnp
from jax import lax
from jax.experimental import pallas as pl
from jax.experimental.pallas import tpu as pltpu
from jax.sharding import PartitionSpec as P

Z_DEV = 16
Y_DEV = 16
NX = 1024
CAP = 64
S_PEER = 2
SWEEPS = 3
HALF = Z_DEV // 2
TILE = (8, 128)
MESH = pl.DeviceIdType.MESH
LOGICAL = pl.DeviceIdType.LOGICAL
F32 = jnp.float32
BF16 = jnp.bfloat16
I32 = jnp.int32


def iota(shape, dim):
    return lax.broadcasted_iota(I32, shape, dim)


def swap_halves(tiles):
    return pltpu.roll(tiles, 4, tiles.ndim - 2)


def low_half(shape):
    return iota(shape, len(shape) - 2) < 4


def neighbour(tiles, parity):
    shape = tiles.shape
    lane, sub = iota(shape, len(shape) - 1), iota(shape, len(shape) - 2) % 4
    if parity == 0:
        near = pltpu.roll(tiles, 1, len(shape) - 1)
        far = pltpu.roll(near, 1, len(shape) - 2)
        edge, end = lane == 0, sub == 0
    else:
        near = pltpu.roll(tiles, 127, len(shape) - 1)
        far = pltpu.roll(near, 7, len(shape) - 2)
        edge, end = lane == 127, sub == 3
    return jnp.where(edge, jnp.where(end, 0.0, far), near)


def by_rows(tiles, parity, function):
    pairs = tiles.reshape(tiles.shape[0] // 2, 2, *TILE)
    done = [function(pairs[:, q], (parity + q) % 2) for q in range(2)]
    return jnp.stack(done, axis=1).reshape(tiles.shape)


def parts(x):
    high = x.astype(BF16)
    return high, (x - high.astype(F32)).astype(BF16)


def deinterleave(guess_ref, start_ref):
    col, row = iota((256, 256), 1), iota((256, 256), 0)
    place = (row == jnp.where(col < 128, 2 * col, 2 * col - 255)).astype(BF16)
    rows = Z_DEV * Y_DEV
    cells = iota((rows, 128), 0)
    even = (cells + cells // Y_DEV) % 2 == 0
    for i in range(4):
        chunk = guess_ref[:, :, 256 * i : 256 * (i + 1)].reshape(rows, 256)
        high, low = parts(chunk)
        split = jnp.dot(high, place, preferred_element_type=F32) + jnp.dot(low, place, preferred_element_type=F32)
        first, second = split[:, :128], split[:, 128:]
        colours = (jnp.where(even, first, second), jnp.where(even, second, first))
        for colour in range(2):
            for z in range(Z_DEV):
                base = ((colour * HALF + z % HALF) * Y_DEV) * 8 + (z // HALF) * 4 + i
                start_ref[pl.ds(base, Y_DEV, stride=8), :] = colours[colour][z * Y_DEV : (z + 1) * Y_DEV]


SIDES = [(1, 1), (1, -1), (-1, 1), (-1, -1), (1, 0), (-1, 0), (0, 1), (0, -1)]
WIDE = 2
ROWS = 7
FULL = (HALF, Y_DEV, *TILE)


def rimmed(width):
    return (HALF + 2 * width, Y_DEV + 2 * width, *TILE)


def edge_shape(width):
    return (2, width, HALF + 2 * width, *TILE)


class Grid:
    def __init__(self):
        self.ns, self.nr = lax.axis_size("slab"), lax.axis_size("row")
        self.slab, self.line = lax.axis_index("slab"), lax.axis_index("row")

    def exists(self, d):
        tests = []
        for step, at, size in ((d[0], self.slab, self.ns), (d[1], self.line, self.nr)):
            if step == 1:
                tests.append(at < size - 1)
            if step == -1:
                tests.append(at > 0)
        return tests[0] if len(tests) == 1 else tests[0] & tests[1]

    def device(self, d):
        return (self.slab + d[0], self.line + d[1])

    def greet_neighbours(self):
        barrier = pltpu.get_barrier_semaphore()
        for d in SIDES:
            @pl.when(self.exists(d))
            def _():
                pl.semaphore_signal(barrier, inc=1, device_id=self.device(d), device_id_type=MESH)

    def await_neighbours(self):
        counts = [
            1 + (at > 0).astype(I32) + (at < size - 1).astype(I32)
            for at, size in ((self.slab, self.ns), (self.line, self.nr))
        ]
        pl.semaphore_wait(pltpu.get_barrier_semaphore(), counts[0] * counts[1] - 1)

    def start(self, pairs):
        for d, copy in pairs:
            @pl.when(self.exists(d))
            def _():
                copy.start()

    def take(self, pairs):
        for d, copy in pairs:
            @pl.when(self.exists((-d[0], -d[1])))
            def _():
                copy.wait_recv()

    def sent(self, pairs):
        for d, copy in pairs:
            @pl.when(self.exists(d))
            def _():
                copy.wait_send()

    def clear(self, pairs):
        for d, dst in pairs:
            @pl.when(jnp.logical_not(self.exists((-d[0], -d[1]))))
            def _():
                dst[...] = jnp.zeros(dst.shape, F32)

    def halo(self, tiles, edge, face, beside=None):
        w = WIDE
        ends = {1: pl.ds(Y_DEV, w), -1: pl.ds(w, w)}
        plan = []
        for d in SIDES:
            side = 0 if d[0] == 1 else 1
            if d[0] == 0:
                dst = tiles.at[pl.ds(w, HALF), pl.ds(0 if d[1] == 1 else Y_DEV + w, w)]
                if beside is not None:
                    dst = beside.at[0 if d[1] == 1 else 1]
                plan.append((d, tiles.at[pl.ds(w, HALF), ends[d[1]]], dst))
            elif d[1] == 0:
                plan.append((d, face.at[side], edge.at[side, pl.ds(0, w), pl.ds(0, HALF)]))
            else:
                dst = edge.at[side, pl.ds(0, w), pl.ds(HALF if d[1] == 1 else HALF + w, w)]
                plan.append((d, tiles.at[pl.ds(HALF if d[0] == 1 else w, w), ends[d[1]]], dst))
        return plan

    def copies(self, plan, send, recv):
        return [
            (d, pltpu.make_async_remote_copy(src, dst, send.at[q], recv.at[q], self.device(d), MESH))
            for q, (d, src, dst) in enumerate(plan)
        ]


def landing(plan):
    return [(d, dst) for d, _, dst in plan]


def pack_top(first, second):
    return jnp.where(low_half(first.shape), swap_halves(first), second)


def pack_bottom(first, second):
    return jnp.where(low_half(first.shape), first, swap_halves(second))


def pack_faces(tiles, face):
    w, half = WIDE, WIDE + HALF
    for p in range(w):
        face[0, p] = pack_top(tiles[HALF + p, w:half], tiles[HALF + p, half : half + HALF])
        face[1, p] = pack_bottom(tiles[w + p, w:half], tiles[w + p, half : half + HALF])


def under(own, corner):
    return swap_halves(jnp.where(low_half(own.shape), own, corner))


def over(own, corner):
    return swap_halves(jnp.where(low_half(own.shape), corner, own))


def rim_planes(tiles, w, p, below, above):
    half = w + HALF
    first, second = slice(w, half), slice(half, half + HALF)
    top, bottom = tiles[HALF + p], tiles[w + p]
    low = low_half((HALF, *TILE))
    up, down = p, HALF + w + p
    tiles[up, first] = jnp.where(low, below[:HALF], swap_halves(top[first]))
    tiles[up, second] = swap_halves(jnp.where(low, top[second], below[:HALF]))
    tiles[down, first] = swap_halves(jnp.where(low, above[:HALF], bottom[first]))
    tiles[down, second] = jnp.where(low, swap_halves(bottom[second]), above[:HALF])
    for y, at in ((slice(0, w), slice(HALF, half)), (slice(Y_DEV + w, Y_DEV + 2 * w), slice(half, half + w))):
        tiles[up, y] = under(top[y], below[at])
        tiles[down, y] = over(bottom[y], above[at])


def rims(tiles, edge):
    for p in range(WIDE):
        rim_planes(tiles, WIDE, p, edge[0, p], edge[1, p])


def bin_kernel(
    brick_in, count_in, cell_in, frac_in, normal_in, weight_in, guess_in, points_ref, v_ref,
    brick_ref, count_ref, cell_ref, frac_ref, normal_ref, weight_ref, guess_ref,
    packed, split, edge, face, load, psend, precv, send, recv,
):
    loads = [
        pltpu.make_async_copy(src, dst, load.at[q])
        for q, (src, dst) in enumerate(
            (
                (guess_in, guess_ref), (brick_in, brick_ref), (count_in, count_ref), (cell_in, cell_ref),
                (frac_in, frac_ref), (normal_in, normal_ref), (weight_in, weight_ref),
            )
        )
    ]
    for copy in loads:
        copy.start()
    grid = Grid()
    peers = grid.ns * grid.nr
    me = grid.slab * grid.nr + grid.line
    barrier = pltpu.get_barrier_semaphore()
    plans = [grid.halo(v_ref.at[c], edge.at[c], face.at[c]) for c in range(2)]
    for plan in plans:
        grid.clear(landing(plan))

    sizes = (4, 4, 2, 4) if peers == 128 else (1, 1, grid.ns, grid.nr)
    strides = [sizes[1] * sizes[2] * sizes[3], sizes[2] * sizes[3], sizes[3], 1]
    shifted = [
        [lax.rem(lax.rem(me // stride, size) + k, size) * stride for k in range(size)]
        for stride, size in zip(strides, sizes)
    ]
    steps = [(z, x, c, y) for z in range(sizes[0]) for x in range(sizes[1]) for c in range(sizes[2]) for y in range(sizes[3])]
    hops = {o: sum(min(k, size - k) for k, size in zip(o, sizes)) for o in steps}
    order = sorted(steps[1:], key=lambda o: -hops[o])

    def peer(o):
        return sum(column[k] for column, k in zip(shifted, o))

    for o in order:
        pl.semaphore_signal(barrier, inc=1, device_id=peer(o), device_id_type=LOGICAL)

    loads[0].wait()
    deinterleave(guess_ref, split)
    for colour in range(2):
        for zp in range(HALF):
            at = (colour * HALF + zp) * Y_DEV * 8
            v_ref[colour, zp + WIDE, WIDE : WIDE + Y_DEV] = split[at : at + Y_DEV * 8, :].reshape(Y_DEV, *TILE)
        pack_faces(v_ref.at[colour], face.at[colour])
    for copy in loads[1:]:
        copy.wait()

    point = iota((CAP, peers), 0)
    live = jnp.concatenate([(point < count_ref[s : s + 1, :]).astype(F32) for s in range(S_PEER)], axis=0)

    def put(r, first, second, mask=None):
        both = jnp.concatenate([first, second], axis=0).astype(F32)
        packed[pl.ds(r, peers, stride=8), :] = (both if mask is None else both * mask).T

    put(0, cell_ref[0], cell_ref[1])
    put(1, frac_ref[0], frac_ref[1])
    for ch in range(3):
        put(2 + ch, normal_ref[0, ch], normal_ref[1, ch], live)
    put(5, weight_ref[0], weight_ref[1], live)
    put(6, *[jnp.broadcast_to(brick_ref[s : s + 1, :], point.shape) for s in range(S_PEER)])

    def rows(t):
        return pl.ds(pl.multiple_of(t * 8, 8), ROWS)

    pl.semaphore_wait(barrier, peers - 1)

    halos = [grid.copies(plans[c], send.at[c], recv.at[c]) for c in range(2)]
    for o in order[:32]:
        t = peer(o)
        pltpu.make_async_remote_copy(packed.at[rows(t)], points_ref.at[rows(me)], psend, precv, t, LOGICAL).start()
    for colour in range(2):
        grid.start(halos[colour][:6])
    for o in order[32:]:
        t = peer(o)
        pltpu.make_async_remote_copy(packed.at[rows(t)], points_ref.at[rows(me)], psend, precv, t, LOGICAL).start()
    for colour in range(2):
        grid.start(halos[colour][6:])
    points_ref[rows(me), :] = packed[rows(me), :]
    for colour in range(2):
        grid.take(halos[colour])
        rims(v_ref.at[colour], edge.at[colour])
    others = pl.ds(0, (peers - 1) * ROWS)
    every = pltpu.make_async_remote_copy(packed.at[others], points_ref.at[others], psend, precv, peer(order[-1]), LOGICAL)
    every.wait_recv()
    every.wait_send()
    for colour in range(2):
        grid.sent(halos[colour])


def splat_kernel(points_ref, rhs_ref, inv_ref, ysend_ref, zsend_ref, csend_ref, acc, brick_v, brick_s, f1, f2, sem):
    sources = points_ref.shape[0] // 8
    brick_v[...] = points_ref[pl.ds(6, sources, stride=8), :].astype(I32)
    copy = pltpu.make_async_copy(brick_v, brick_s, sem)
    copy.start()

    def clear(b, _):
        acc[pl.ds(b * 8, 8)] = jnp.zeros((8, 32, 128), F32)
        return 0

    lax.fori_loop(0, Z_DEV * Y_DEV // 8, clear, 0)
    copy.wait()

    lane = iota(TILE, 1)
    left = lane < CAP
    rank = iota(TILE, 0)
    wide_rank = iota((128, 128), 0)

    def group(g, _):
        cell, frac, n0, n1, n2, w, brick = [points_ref[pl.ds(g * 64 + r, 8, stride=8), :] for r in range(7)]
        cell, brick = cell.astype(I32), brick.astype(I32)
        parity, k = cell & 1, cell >> 1
        even = parity == 0
        wl = 0.5 * (0.5 - frac) * (0.5 - frac)
        wm = 0.75 - frac * frac
        wh = 0.5 * (0.5 + frac) * (0.5 + frac)
        beside = jnp.where(even, wh, wl)
        beyond = jnp.where(even, wl, wh)
        k2 = jnp.where(even, k - 1, k + 1)
        zl, yl = brick >> 4, brick & 15
        side = (parity + zl + yl + (zl >> 3)) & 1
        h1 = side * 4 + (k >> 7)
        h2 = (1 - side) * 4 + (k >> 7)
        inside = (k2 >= 0) & (k2 < NX // 2)
        h3 = jnp.where(inside, (1 - side) * 4 + (k2 >> 7), -1)
        none = jnp.full(TILE, -1, I32)
        zero = jnp.zeros(TILE, F32)

        def swap(x):
            return pltpu.roll(x, 64, 1)

        def both(x, y):
            return (jnp.where(left, x, swap(y)), jnp.where(left, swap(x), y))

        lanes_ = both(k & 127, k2 & 127)
        ha, hb = both(h1, h3), both(h2, none)
        wa, wb = both(wm, beyond), both(beside, zero)
        vals = [both(v, v) for v in (n0, n1, n2, w)]
        for r in range(8):
            weights, onehots = [], []
            for s in range(S_PEER):
                def row(x):
                    return x[s][r : r + 1, :]

                unit = jnp.where(rank == row(ha), row(wa), jnp.where(rank == row(hb), row(wb), 0.0))
                weights.append(jnp.concatenate(parts(jnp.concatenate([unit * row(v) for v in vals], axis=0)), axis=0))
                onehots.append((wide_rank == row(lanes_)).astype(F32).astype(BF16))
            apart = jnp.zeros(weights[0].shape, BF16)
            diagonal = jnp.concatenate(
                [jnp.concatenate([weights[0], apart], axis=1), jnp.concatenate([apart, weights[1]], axis=1)], axis=0
            )
            out = lax.dot_general(
                diagonal, jnp.concatenate(onehots, axis=1), (((1,), (1,)), ((), ())), preferred_element_type=F32
            )
            for s in range(S_PEER):
                b = brick_s[g * 8 + r, s * CAP]
                acc[b] = acc[b] + (out[s * 64 : s * 64 + 32] + out[s * 64 + 32 : s * 64 + 64])
        return 0

    lax.fori_loop(0, sources // 8, group, 0, unroll=min(16, sources // 8))

    low = low_half((Y_DEV, *TILE))

    def fields(zp, ch):
        one = acc[pl.ds(zp * Y_DEV, Y_DEV), ch * 8 : ch * 8 + 8, :]
        two = acc[pl.ds((zp + HALF) * Y_DEV, Y_DEV), ch * 8 : ch * 8 + 8, :]
        return jnp.where(low, one, two), swap_halves(jnp.where(low, two, one))

    nil = jnp.zeros((1, *TILE), F32)
    for colour in range(2):
        for zp in range(HALF):
            f1[colour, zp, 0:1] = nil
            f1[colour, zp, Y_DEV + 1 : Y_DEV + 2] = nil

    def planes(pair, _):
        for odd in range(2):
            zp = pair * 2 + odd
            x = fields(zp, 0)
            y = fields(zp, 1)
            z = fields(zp, 2)
            d = fields(zp, 3)
            for colour in range(2):
                def slope(tiles, parity):
                    other = neighbour(tiles, parity)
                    return tiles - other if parity == 0 else other - tiles

                rhs_ref[colour, zp] = by_rows(x[1 - colour], (odd + colour) % 2, slope)
                f1[colour, zp, 1 : Y_DEV + 1] = y[colour]
                f2[colour, zp + 1] = z[colour]
                inv_ref[colour, zp] = 1.0 / (32.0 + 48.0 * d[colour])
                ysend_ref[0, (26, 16)[colour] + zp] = y[colour][0]
                ysend_ref[1, (26, 16)[colour] + zp] = y[colour][Y_DEV - 1]
        return 0

    lax.fori_loop(0, HALF // 2, planes, 0)
    zsend_ref[0, 16:32] = acc[0:Y_DEV, 16:24, :]
    zsend_ref[1, 16:32] = acc[(Z_DEV - 1) * Y_DEV :, 16:24, :]
    for colour in range(2):
        f2[colour, 0] = swap_halves(jnp.where(low, f2[colour, HALF], 0.0))
        f2[colour, HALF + 1] = swap_halves(jnp.where(low, 0.0, f2[colour, 1]))

    def finish(zp, _):
        for colour in range(2):
            o = 1 - colour
            spread = rhs_ref[colour, zp] + f1[o, zp, 2:] - f1[o, zp, :-2] + f2[o, zp + 2] - f2[o, zp]
            rhs_ref[colour, zp] = -6.0 * spread
        return 0

    lax.fori_loop(0, HALF, finish, 0)
    ends = (0, Y_DEV - 1)
    for s, y in enumerate(ends):
        ysend_ref[s, 0:HALF] = rhs_ref[0, :, y]
        ysend_ref[s, HALF : 2 * HALF] = inv_ref[0, :, y]
        for t in range(2):
            ysend_ref[s, 24 + t] = zsend_ref[t, 16 + y]
    for t, zp in enumerate((0, HALF - 1)):
        pack = pack_top if t == 1 else pack_bottom
        for q, ref in enumerate((rhs_ref, inv_ref)):
            zsend_ref[t, q * HALF : (q + 1) * HALF] = pack(ref[0, zp, :HALF], ref[0, zp, HALF:])
        for s, y in enumerate(ends):
            slope = f1[1, zp, y + 1]
            zsend_ref[t, 32 + s] = slope
            for q, tile in enumerate((rhs_ref[0, zp, y], inv_ref[0, zp, y], slope, zsend_ref[t, 16 + y])):
                csend_ref[2 * t + s, q] = tile


def relax_kernel(
    rhs_in, inv_in, start_ref, ysend_ref, zsend_ref, csend_ref, out_ref,
    v, edge, face, beside, red, red_inv, black, yin, zin, cin, send, recv, fsend, frecv, lsend, lrecv,
):
    grid = Grid()
    grid.greet_neighbours()
    w, end = WIDE, WIDE + Y_DEV
    versions = [start_ref.at[0], start_ref.at[1]] + [v.at[n] for n in range(2 * SWEEPS - 1)]
    plans = [
        grid.halo(versions[n + 2], edge.at[n], face.at[n], beside.at[n // 2] if n % 2 == 0 else None)
        for n in range(2 * SWEEPS - 2)
    ]
    for plan in plans:
        grid.clear(landing(plan))
    fields, late = [], []
    for d in SIDES:
        to = [(int(x == 1), int(x != 1)) for x in d]
        if d[0] == 0:
            for plan, part in ((fields, pl.ds(0, 26)), (late, pl.ds(26, 8))):
                plan.append((d, ysend_ref.at[to[1][0], part], yin.at[to[1][1], part]))
        elif d[1] == 0:
            fields.append((d, zsend_ref.at[to[0][0]], zin.at[to[0][1]]))
        else:
            fields.append((d, csend_ref.at[2 * to[0][0] + to[1][0]], cin.at[2 * to[0][1] + to[1][1]]))
    grid.clear(landing(fields) + landing(late))
    for zp in range(HALF):
        red[zp + 1, 1 : Y_DEV + 1] = rhs_in[0, zp]
        red_inv[zp + 1, 1 : Y_DEV + 1] = inv_in[0, zp]
        black[zp] = rhs_in[1, zp]

    def update(step, plane, y, count):
        plane, parity = (plane, plane) if isinstance(plane, int) else plane
        same, opp, colour = versions[step], versions[step + 1], step % 2
        if colour == 0:
            right, scale = red[plane - 1, y - 1 : y - 1 + count], red_inv[plane - 1, y - 1 : y - 1 + count]
        else:
            right, scale = black[plane - w, y - w : y - w + count], inv_in[1, plane - w, y - w : y - w + count]
        s1 = same[plane - 1, y - 1 : y + count + 1] + same[plane + 1, y - 1 : y + count + 1]
        o1 = opp[plane - 1, y - 1 : y + count + 1] + opp[plane + 1, y - 1 : y + count + 1]
        s0 = same[plane, y - 1 : y + count + 1]
        around = s1[1:-1] + s0[:-2] + s0[2:]
        diagonal = s1[:-2] + s1[2:]
        across = 2.0 * around + (o1[:-2] + o1[2:])
        total = right + 2.0 * diagonal + across
        value = (total + by_rows(across, (parity + y + colour) % 2, neighbour)) * scale
        if step == 2 * SWEEPS - 1:
            out_ref[1, plane - w, y - w : y - w + count] = value
        else:
            versions[step + 2][plane, y : y + count] = value

    def inside(step, first, planes, y, count):
        def pair(i, _):
            for odd in range(2):
                update(step, (i * 2 + first + odd, first + odd), y, count)
            return 0

        lax.fori_loop(0, planes // 2, pair, 0)

    def red_inside(sweep):
        inside(2 * sweep, w + 1, HALF - 2, w + 1, Y_DEV - 2)

    def red_faces(sweep):
        for plane in (w, w + HALF - 1):
            update(2 * sweep, plane, w - 1, Y_DEV + 2)
        for plane in range(w + 1, w + HALF - 1):
            for y in (w - 1, end - 1):
                update(2 * sweep, plane, y, 2)

    def red_ring(sweep):
        for plane in (w - 1, w + HALF):
            update(2 * sweep, plane, w - 1, Y_DEV + 2)

    def black_faces(sweep):
        for plane in (w, w + HALF - 1):
            update(2 * sweep + 1, plane, w, Y_DEV)
        for plane in range(w + 1, w + HALF - 1):
            for y in (w, end - 2):
                update(2 * sweep + 1, plane, y, 2)

    def black_second(sweep):
        for plane in (w + 1, w + HALF - 2):
            update(2 * sweep + 1, plane, w + 2, Y_DEV - 4)

    def black_inside(sweep):
        inside(2 * sweep + 1, w + 2, HALF - 4, w + 2, Y_DEV - 4)

    red_inside(0)
    grid.await_neighbours()
    pairs = grid.copies(fields, fsend, frecv)
    tail = grid.copies(late, lsend, lrecv)
    grid.start(pairs + tail)
    sent = [pairs, tail]
    grid.take(pairs)

    for tiles, q in ((red, 0), (red_inv, 1)):
        for s, y in enumerate((0, Y_DEV + 1)):
            tiles[1 : HALF + 1, y] = yin[s, q * HALF : (q + 1) * HALF]
        sides = [
            jnp.concatenate([zin[t, q * HALF : (q + 1) * HALF], cin[2 * t, q : q + 1], cin[2 * t + 1, q : q + 1]], axis=0)
            for t in range(2)
        ]
        rim_planes(tiles, 1, 0, sides[0], sides[1])

    def slopes(own, below, above):
        return jnp.concatenate([under(own[HALF - 1 :], below), own, over(own[:1], above)], axis=0)

    inner_y = [slopes(ysend_ref[s, 16:24], zin[0, 32 + s : 33 + s], zin[1, 32 + s : 33 + s]) for s in range(2)]
    outer_y = [slopes(yin[s, 16:24], cin[s, 2:3], cin[2 + s, 2:3]) for s in range(2)]
    red[:, 0] -= 6.0 * inner_y[0]
    red[:, 1] += 6.0 * outer_y[0]
    red[:, Y_DEV] -= 6.0 * outer_y[1]
    red[:, Y_DEV + 1] += 6.0 * inner_y[1]

    low = low_half((Y_DEV + 2, *TILE))
    inner_z = [
        jnp.concatenate([yin[0, 24 + t : 25 + t], zsend_ref[t, 16:32], yin[1, 24 + t : 25 + t]], axis=0) for t in range(2)
    ]
    outer_z = [
        jnp.concatenate([cin[2 * t, 3:4], zin[t, 16:32], cin[2 * t + 1, 3:4]], axis=0) for t in range(2)
    ]
    red[0] -= jnp.where(low, 6.0 * swap_halves(inner_z[0]), 0.0)
    red[1] += jnp.where(low, 6.0 * outer_z[0], 0.0)
    red[HALF] -= jnp.where(low, 0.0, 6.0 * outer_z[1])
    red[HALF + 1] += jnp.where(low, 0.0, 6.0 * swap_halves(inner_z[1]))
    black[0] += jnp.where(low[1:-1], 6.0 * swap_halves(zin[0, 16:32]), 0.0)
    black[HALF - 1] -= jnp.where(low[1:-1], 0.0, 6.0 * swap_halves(zin[1, 16:32]))

    for sweep in range(SWEEPS):
        final = sweep == SWEEPS - 1
        news = (2 * sweep, 2 * sweep + 1)
        flying = []

        def launch(n, between):
            pairs = grid.copies(plans[n], send.at[n], recv.at[n])
            between(sweep)
            pack_faces(versions[n + 2], face.at[n])
            grid.start(pairs)
            flying.append(pairs)

        red_faces(sweep)
        if not final:
            launch(news[0], lambda _: None)
        red_ring(sweep)
        if sweep == 0:
            grid.take(tail)
            black[:, 0] += 6.0 * yin[0, 26:34]
            black[:, Y_DEV - 1] -= 6.0 * yin[1, 26:34]
        black_faces(sweep)
        if not final:
            launch(news[1], black_second)
        else:
            black_second(sweep)
        black_inside(sweep)
        if not final:
            red_inside(sweep + 1)
            for n, pairs in zip(news, flying):
                grid.take(pairs)
                if n % 2 == 0:
                    for s, y in enumerate((0, end)):
                        versions[n + 2][w : w + HALF, y : y + w] = beside[n // 2, s]
                rims(versions[n + 2], edge.at[n])
            sent += flying

    for zp in range(HALF):
        out_ref[0, zp] = versions[2 * SWEEPS][zp + w, w:end]
    for pairs in sent:
        grid.sent(pairs)


def interleave_kernel(in_ref, out_hbm, out_ref, sem):
    copies = []
    col, row = iota((256, 256), 1), iota((256, 256), 0)
    place = (col == jnp.where(row < 128, 2 * row, 2 * row - 255)).astype(BF16)
    rows = Z_DEV * Y_DEV
    cells = iota((rows, 128), 0)
    even = (cells + cells // Y_DEV) % 2 == 0
    for i in range(4):
        colours = []
        for colour in range(2):
            base = [((colour * HALF + z % HALF) * Y_DEV) * 8 + (z // HALF) * 4 + i for z in range(Z_DEV)]
            colours.append(jnp.concatenate([in_ref[pl.ds(b, Y_DEV, stride=8), :] for b in base], axis=0))
        red, black = colours
        both = jnp.concatenate([jnp.where(even, red, black), jnp.where(even, black, red)], axis=1)
        high, low = parts(both)
        merged = jnp.dot(high, place, preferred_element_type=F32) + jnp.dot(low, place, preferred_element_type=F32)
        out_ref[i] = merged.reshape(Z_DEV, Y_DEV, 256)
        copy = pltpu.make_async_copy(out_ref.at[i], out_hbm.at[:, :, pl.ds(256 * i, 256)], sem.at[i])
        copy.start()
        copies.append(copy)
    for copy in copies:
        copy.wait()


VM = pl.BlockSpec(memory_space=pltpu.VMEM)


def call(kernel, outs, scratch, specs, limit, out=VM, **params):
    return pl.pallas_call(
        kernel,
        out_shape=outs,
        in_specs=specs,
        out_specs=jax.tree.map(lambda _: out, outs),
        scratch_shapes=scratch,
        compiler_params=pltpu.CompilerParams(vmem_limit_bytes=limit << 20, **params),
    )


def shards(slot_brick, slot_count, point_cell, point_frac, point_normal, point_weight, guess):
    peers = point_cell.shape[1]
    full = jax.ShapeDtypeStruct((2, *FULL), F32)
    steps = 2 * SWEEPS - 1

    def last(x):
        return jnp.moveaxis(x[0], 0, -1)

    args = (last(slot_brick), last(slot_count), last(point_cell), last(point_frac), last(point_normal), last(point_weight), guess)
    points, start = call(
        bin_kernel,
        (jax.ShapeDtypeStruct((peers * 8, 128), F32), jax.ShapeDtypeStruct((2, *rimmed(WIDE)), F32)),
        [pltpu.VMEM(a.shape, a.dtype) for a in args]
        + [
            pltpu.VMEM((peers * 8, 128), F32),
            pltpu.VMEM((2 * HALF * Y_DEV * 8, 128), F32),
            pltpu.VMEM((2, *edge_shape(WIDE)), F32),
            pltpu.VMEM((2, 2, WIDE, HALF, *TILE), F32),
            pltpu.SemaphoreType.DMA((7,)),
            pltpu.SemaphoreType.DMA,
            pltpu.SemaphoreType.DMA,
            pltpu.SemaphoreType.DMA((2, 8)),
            pltpu.SemaphoreType.DMA((2, 8)),
        ],
        [pl.BlockSpec(memory_space=pltpu.HBM)] * 7,
        24,
        collective_id=0,
        has_side_effects=True,
    )(*[pltpu.with_memory_space_constraint(a, pltpu.HBM) for a in args])
    outs = (
        full,
        full,
        jax.ShapeDtypeStruct((2, 34, *TILE), F32),
        jax.ShapeDtypeStruct((2, 34, *TILE), F32),
        jax.ShapeDtypeStruct((4, 4, *TILE), F32),
    )
    rhs, inv, ysend, zsend, csend = call(
        splat_kernel,
        outs,
        [
            pltpu.VMEM((Z_DEV * Y_DEV, 32, 128), F32),
            pltpu.VMEM((peers, 128), I32),
            pltpu.SMEM((peers, 128), I32),
            pltpu.VMEM((2, HALF, Y_DEV + 2, *TILE), F32),
            pltpu.VMEM((2, HALF + 2, Y_DEV, *TILE), F32),
            pltpu.SemaphoreType.DMA,
        ],
        [VM],
        32,
    )(points)
    relaxed = call(
        relax_kernel,
        full,
        [
            pltpu.VMEM((steps, *rimmed(WIDE)), F32),
            pltpu.VMEM((steps - 1, *edge_shape(WIDE)), F32),
            pltpu.VMEM((steps - 1, 2, WIDE, HALF, *TILE), F32),
            pltpu.VMEM((SWEEPS - 1, 2, HALF, WIDE, *TILE), F32),
            pltpu.VMEM(rimmed(1), F32),
            pltpu.VMEM(rimmed(1), F32),
            pltpu.VMEM(FULL, F32),
            pltpu.VMEM((2, 34, *TILE), F32),
            pltpu.VMEM((2, 34, *TILE), F32),
            pltpu.VMEM((4, 4, *TILE), F32),
            pltpu.SemaphoreType.DMA((steps - 1, 8)),
            pltpu.SemaphoreType.DMA((steps - 1, 8)),
            pltpu.SemaphoreType.DMA((8,)),
            pltpu.SemaphoreType.DMA((8,)),
            pltpu.SemaphoreType.DMA((2,)),
            pltpu.SemaphoreType.DMA((2,)),
        ],
        [VM] * 6,
        32,
        collective_id=1,
        has_side_effects=True,
    )(rhs, inv, start, ysend, zsend, csend)
    return call(
        interleave_kernel,
        jax.ShapeDtypeStruct((Z_DEV, Y_DEV, NX), F32),
        [pltpu.VMEM((4, Z_DEV, Y_DEV, 256), F32), pltpu.SemaphoreType.DMA((4,))],
        [VM],
        16,
        out=pl.BlockSpec(memory_space=pltpu.HBM),
    )(relaxed.reshape(-1, 128))


def solution(mesh):
    placed = (
        P(("slab", "row"), None, None),
        P(("slab", "row"), None, None),
        P(("slab", "row"), None, None, None),
        P(("slab", "row"), None, None, None),
        P(("slab", "row"), None, None, None, None),
        P(("slab", "row"), None, None, None),
        P("slab", "row", None),
    )
    return jax.shard_map(
        shards, mesh=mesh, in_specs=placed, out_specs=P("slab", "row", None), check_vma=False
    )
```
